512 devices in a mesh: seq: 16 (over z), ch: 32 (over x, y, core).
Axes of the slice: x: 4, y: 4, z: 16, core: 2. Of those that a mesh axis runs over, the one named last changes fastest.
Arguments:
- inputs: bfloat16 [4096, 8192], P('seq', 'ch'), may hold values from -6 to 6
- w_in: bfloat16 [3, 8192, 8192], P(None, 'seq', 'ch'), may hold values from -0.0625 to 0.0625
- short_filter: float32 [3, 3, 8192], P(None, None, 'ch'), may hold values from -3 to 3
- rates: float32 [16, 8192], P(None, 'ch'), may hold values from 2.4414063e-05 to 0.05
- residues: float32 [16, 8192], P(None, 'ch'), may hold values from -3 to 3
- skip: float32 [8192], P('ch'), may hold values from -3 to 3
Outputs:
- gated: bfloat16 [4096, 8192], P('seq', 'ch')
The draws below stay inside these ranges and needn't reach their ends.
All inputs are finite; a program needn't handle non-finite values.
Results may differ from the reference program's by a relative error of at most 0.0065.
Values may be sent and summed in bfloat16 or wider, within the bound.
A program may use at most 64 MiB of HBM per device.

```python
import math
import jax
import jax.numpy as jnp
from jax import lax

D = 8192
MODES = 16
TAPS = 3
TOKENS = 4096


def block_levels(key, dims, pieces, low, largest):
    gain = 1.0
    for axis_at, parts in pieces:
        draws = jax.random.uniform(jax.random.fold_in(jax.random.fold_in(key, 6), axis_at), (parts,), jnp.float32, low / len(pieces), largest / len(pieces))
        gain = gain * jnp.repeat(jnp.exp(draws), dims[axis_at] // parts).reshape((-1,) + (1,) * (len(dims) - 1 - axis_at))
    return gain


def scatter_about(stream_key, extent, scale, most, split=(), kind=jnp.bfloat16):
    result = scale * jax.random.normal(stream_key, extent, jnp.float32)
    if split:
        result = result * block_levels(stream_key, extent, split, -0.22, 0.18)
    return jnp.clip(result, -most, most).astype(kind)


def setup_inputs(seed: int = 0) -> dict:
    streams_of = jax.random.split(jax.random.key(seed), 7)
    inputs = scatter_about(streams_of[0], (TOKENS, D), 1.0, 6.0, ((0, 16), (1, 32)))
    w_in = scatter_about(streams_of[1], (3, D, D), D ** -0.5, 0.0625, ((1, 16), (2, 32)))
    short_filter = scatter_about(streams_of[2], (3, TAPS, D), 0.6, 3.0, ((2, 32),), jnp.float32)
    rates = jnp.clip(jnp.exp(math.log(0.05) - 7.624619 * jax.random.uniform(streams_of[3], (MODES, D), jnp.float32) ** block_levels(streams_of[3], (MODES, D), ((1, 32),), -0.2, 0.2)), 2.441406286379788e-05, 0.05)
    residues = scatter_about(streams_of[4], (MODES, D), 0.5, 3.0, ((1, 32),), jnp.float32)
    skip = scatter_about(streams_of[5], (D,), 0.5, 3.0, ((0, 32),), jnp.float32)
    return {"inputs": inputs, "w_in": w_in, "short_filter": short_filter, "rates": rates, "residues": residues, "skip": skip}


def reference(inputs, w_in, short_filter, rates, residues, skip):
    proj = jnp.stack([jnp.dot(inputs, w_in[i], preferred_element_type=jnp.float32).astype(jnp.bfloat16) for i in range(3)])
    padded = jnp.concatenate([jnp.zeros((3, TAPS - 1, D), jnp.bfloat16), proj], axis=1).astype(jnp.float32)
    mixed = jnp.zeros((3, TOKENS, D), jnp.float32)
    for j in range(TAPS):
        mixed = mixed + short_filter[:, j, None, :] * padded[:, TAPS - 1 - j:TAPS - 1 - j + TOKENS, :]
    query, key, value = (mixed[0], mixed[1], mixed[2])
    drive = key * value
    factor = jnp.exp(-rates)
    scaled = residues * jnp.sqrt(1.0 - jnp.exp(-2.0 * rates))

    def advance(state, entry):
        state = factor * state + entry[None, :]
        return (state, lax.optimization_barrier(jnp.sum(scaled * state, axis=0)))
    _, longconv = lax.scan(advance, jnp.zeros((MODES, D), jnp.float32), drive)
    return (query * (longconv + skip[None, :] * drive)).astype(jnp.bfloat16)
```

```python
import functools

import jax
import jax.numpy as jnp
from jax import lax
from jax.experimental import pallas as pl
from jax.experimental.pallas import tpu as pltpu
from jax.sharding import PartitionSpec as P

MESH = pl.DeviceIdType.MESH
Z = 16
S = 4
TOK = 256
LANE = 128
MODES = 16
TAPS = 3


def kernel(
    x_ref, w_ref, sf_ref, rates_ref, res_ref, skip_ref, out_ref,
    wg, xg, acc, pad, halo, query, drive, est, ysum,
    xy_s, xy_r, xx_s, xx_r, xc_s, xc_r, w_s, w_r, h_s, h_r, e_s, e_r,
):
    z = lax.axis_index("seq")
    ch = lax.axis_index("ch")
    core = ch % 2
    y = (ch // 2) % S
    x = ch // (2 * S)
    c = ch // 2

    def z_at(d):
        return ((z + d) % Z, ch)

    def y_at(d):
        return (z, (x * S + (y + d) % S) * 2 + core)

    def x_at(d):
        return (z, (((x + d) % S) * S + y) * 2 + core)

    other = (z, c * 2 + 1 - core)

    barrier = pltpu.get_barrier_semaphore()
    partners = [z_at(d) for d in range(1, Z)] + [y_at(d) for d in range(1, S)]
    partners += [x_at(d) for d in range(1, S)] + [other]
    for p in partners:
        pl.semaphore_signal(barrier, inc=1, device_id=p, device_id_type=MESH)
    pl.semaphore_wait(barrier, len(partners))

    started = []

    def remote(src, dst, ss, rs, dev):
        return pltpu.make_async_remote_copy(
            src_ref=src, dst_ref=dst, send_sem=ss, recv_sem=rs, device_id=dev, device_id_type=MESH
        )

    def go(copy):
        copy.start()
        started.append(copy)

    def valid(way, k, p):
        return k < Z // 2 or p == way

    def slot(way, h, k, p):
        return wg.at[h, (z - k if way == 0 else z + k) % Z, p]

    def w_copy(way, h, k, p, at):
        ref = slot(way, h, at, p)
        return remote(ref, ref, w_s.at[way, h, k, p], w_r.at[way, h, k, p], z_at(1 if way == 0 else -1))

    def own(h):
        for p in range(2):
            wg[h, z, p] = w_ref[:, pl.ds(256 * p, 256), pl.ds(LANE * h, LANE)]

    def inject(h):
        for p in range(2):
            for way in range(2):
                go(w_copy(way, h, 0, p, 0))

    own(0)
    inject(0)
    xg[core, c] = x_ref[...]
    for d in range(1, S):
        go(remote(xg.at[core, c], xg.at[core, c], xy_s.at[d - 1], xy_r.at[d - 1], y_at(d)))
    own(1)

    def x_second():
        for d in range(1, S):
            ref = xg.at[core, x * S + (y - d) % S]
            remote(ref, ref, xy_s.at[d - 1], xy_r.at[d - 1], y_at(d)).wait_recv()
        mine = xg.at[core, pl.ds(x * S, S)]
        for d in range(1, S):
            go(remote(mine, mine, xx_s.at[d - 1], xx_r.at[d - 1], x_at(d)))
        go(remote(mine, mine, xc_s.at[0], xc_r.at[0], other))

    def x_third():
        for d in range(1, S):
            ref = xg.at[core, pl.ds(((x - d) % S) * S, S)]
            remote(ref, ref, xx_s.at[d - 1], xx_r.at[d - 1], x_at(d)).wait_recv()
            go(remote(ref, ref, xc_s.at[d], xc_r.at[d], other))

    def x_last():
        for d in range(S):
            ref = xg.at[1 - core, pl.ds(((x - d) % S) * S, S)]
            remote(ref, ref, xc_s.at[d], xc_r.at[d], other).wait_recv()

    def project(h):
        acc[...] = jnp.zeros_like(acc)

        @pl.loop(0, Z)
        def _(s):
            for i in range(3):
                total = acc[i]
                for p in range(2):
                    total += jnp.dot(xg[p, s], wg[h, s, p, i], preferred_element_type=jnp.float32)
                acc[i] = total

    def halo_copy(h):
        return remote(pad.at[h, :, pl.ds(TOK, 8)], halo.at[h], h_s.at[h], h_r.at[h], z_at(1))

    def part1(h):
        for i in range(3):
            pad[h, i, 8:, :] = acc[i].astype(jnp.bfloat16).astype(jnp.float32)
        go(halo_copy(h))

    def lanes(h):
        return pl.ds(LANE * h, LANE)

    def state_copy(h, d, src, to):
        return remote(est.at[h, src], est.at[h, src], e_s.at[h, d - 1], e_r.at[h, d - 1], to)

    def part2(h):
        halo_copy(h).wait_recv()
        first = (z > 0).astype(jnp.float32)
        mixed = []
        for i in range(3):
            pad[h, i, 0:8, :] = halo[h, i] * first
            total = jnp.zeros((TOK, LANE), jnp.float32)
            for j in range(TAPS):
                total += sf_ref[i, pl.ds(j, 1), lanes(h)] * pad[h, i, 8 - j : 8 - j + TOK, :]
            mixed.append(total)
        query[h] = mixed[0]
        drive[h] = mixed[1] * mixed[2]
        r = rates_ref[:, lanes(h)]
        f8 = jnp.exp(-8.0 * r)
        steps = [jnp.broadcast_to(f8[m : m + 1, :], (8, LANE)) for m in range(MODES)]

        def one(g, states):
            d = drive[h, pl.ds(pl.multiple_of(g * 8, 8), 8), :]
            return tuple(s * f + d for s, f in zip(states, steps))

        states = lax.fori_loop(0, TOK // 8, one, tuple(jnp.zeros((8, LANE), jnp.float32) for _ in range(MODES)))
        left = 7.0 - lax.broadcasted_iota(jnp.int32, (8, LANE), 0).astype(jnp.float32)
        for m in range(MODES):
            weight = jnp.exp(-r[m : m + 1, :] * left)
            est[h, z, pl.ds(m, 1), :] = jnp.sum(states[m] * weight, axis=0, keepdims=True)
        for d in range(1, Z):
            go(state_copy(h, d, z, z_at(d)))

    def part3(h):
        for d in range(1, Z):
            state_copy(h, d, (z - d) % Z, z_at(d)).wait_recv()
        r = rates_ref[:, lanes(h)]
        block = jnp.exp(-float(TOK) * r)
        entering = jnp.zeros((MODES, LANE), jnp.float32)
        for s in range(Z - 1):
            entering = jnp.where(s < z, entering * block + est[h, s], entering)
        factor = jnp.exp(-r)
        scaled = res_ref[:, lanes(h)] * jnp.sqrt(1.0 - jnp.exp(-2.0 * r))
        fa, fb, sa, sb = factor[:8], factor[8:], scaled[:8], scaled[8:]

        def one(g, state):
            a, b = state
            base = pl.multiple_of(g * 8, 8)
            for t in range(8):
                d = drive[h, pl.ds(base + t, 1), :]
                a = a * fa + d
                b = b * fb + d
                ysum[pl.ds(pl.multiple_of((base + t) * 8, 8), 8), :] = a * sa + b * sb
            return a, b

        lax.fori_loop(0, TOK // 8, one, (entering[:8], entering[8:]))
        total = ysum[pl.ds(0, TOK, stride=8), :]
        for i in range(1, 8):
            total += ysum[pl.ds(i, TOK, stride=8), :]
        gated = query[h] * (total + skip_ref[:, lanes(h)] * drive[h])
        out_ref[:, lanes(h)] = gated.astype(jnp.bfloat16)

    for step in range(Z):
        h, k = step // (Z // 2), step % (Z // 2) + 1
        for p in range(2):
            for way in range(2):
                if valid(way, k, p):
                    w_copy(way, h, k - 1, p, k).wait_recv()
                    if k < Z // 2 and valid(way, k + 1, p):
                        go(w_copy(way, h, k, p, k))
        if h == 0 and k == Z // 2 - 1:
            inject(1)
        if step == 0:
            x_second()
        if step == 4:
            x_third()
        if step == 5:
            x_last()
        if step == 7:
            project(0)
            part1(0)
        if step == 9:
            part2(0)
        if step == 11:
            part3(0)
    project(1)
    part1(1)
    part2(1)
    part3(1)
    for copy in started:
        copy.wait_send()


def per_device(inputs, w_in, short_filter, rates, residues, skip):
    vmem = pl.BlockSpec(memory_space=pltpu.VMEM)
    dma = pltpu.SemaphoreType.DMA
    f32, bf16 = jnp.float32, jnp.bfloat16
    return pl.pallas_call(
        kernel,
        out_shape=jax.ShapeDtypeStruct(inputs.shape, jnp.bfloat16),
        in_specs=[vmem] * 6,
        out_specs=vmem,
        scratch_shapes=[
            pltpu.VMEM((2, Z, 2, 3, 256, LANE), bf16),
            pltpu.VMEM((2, 16, TOK, 256), bf16),
            pltpu.VMEM((3, TOK, LANE), f32),
            pltpu.VMEM((2, 3, TOK + 8, LANE), f32),
            pltpu.VMEM((2, 3, 8, LANE), f32),
            pltpu.VMEM((2, TOK, LANE), f32),
            pltpu.VMEM((2, TOK, LANE), f32),
            pltpu.VMEM((2, Z, MODES, LANE), f32),
            pltpu.VMEM((TOK * 8, LANE), f32),
            dma((3,)), dma((3,)), dma((3,)), dma((3,)), dma((4,)), dma((4,)),
            dma((2, 2, 8, 2)), dma((2, 2, 8, 2)), dma((2,)), dma((2,)),
            dma((2, Z - 1)), dma((2, Z - 1)),
        ],
        compiler_params=pltpu.CompilerParams(
            collective_id=0, has_side_effects=True, vmem_limit_bytes=48 * 2**20
        ),
    )(inputs, w_in, short_filter, rates, residues, skip.reshape(1, -1))


def solution(mesh):
    in_specs = (
        P("seq", "ch"),
        P(None, "seq", "ch"),
        P(None, None, "ch"),
        P(None, "ch"),
        P(None, "ch"),
        P("ch"),
    )
    return jax.shard_map(
        per_device, mesh=mesh, in_specs=in_specs, out_specs=P("seq", "ch"), check_vma=False
    )
```

```python
import functools

import jax
import jax.numpy as jnp
from jax import lax
from jax.experimental import pallas as pl
from jax.experimental.pallas import tpu as pltpu
from jax.sharding import PartitionSpec as P

MESH = pl.DeviceIdType.MESH
Z = 16
S = 4
TOK = 256
LANE = 128
MODES = 16
TAPS = 3


CHUNKS = ((0, 2), (2, 2), (4, 4), (8, 4), (12, 4))
SCALE = 2.0**16


def need_slot(tau):
    ahead = (tau - 1) % Z + 1
    late = (ahead - 1) // (Z // 2)
    return (1 - late) * (Z - 2 * ahead) + late * (2 * ahead - Z - 1)


def coded(total):
    return (total * jnp.abs(total) * (total * total)).astype(jnp.bfloat16)


def plain(sent):
    fourth = sent.astype(jnp.float32)
    root = lax.rsqrt(jnp.maximum(jnp.abs(fourth), 1e-37))
    return fourth * root * root * lax.rsqrt(root)


def kernel(
    x_ref, w_ref, sf_ref, rates_ref, res_ref, skip_ref, out_ref,
    xs, xg, ring, part, acc, pad, halo, query, drive, est, ysum,
    sc_s, sc_r, xy_s, xy_r, xx_s, xx_r, xc_s, xc_r, p_s, p_r, h_s, h_r, e_s, e_r,
):
    z = lax.axis_index("seq")
    ch = lax.axis_index("ch")
    core = ch % 2
    y = (ch // 2) % S
    x = ch // (2 * S)
    c = ch // 2

    def z_at(d):
        return ((z + d) % Z, ch)

    def y_at(d):
        return (z, (x * S + (y + d) % S) * 2 + core)

    def x_at(d):
        return (z, (((x + d) % S) * S + y) * 2 + core)

    other = (z, c * 2 + 1 - core)
    barrier = pltpu.get_barrier_semaphore()

    def greet(device):
        pl.semaphore_signal(barrier, inc=1, device_id=device, device_id_type=MESH)

    partners = [z_at(d) for d in range(1, Z)] + [y_at(d) for d in range(1, S)]
    partners += [x_at(d) for d in range(1, S)] + [other]
    partners += [((z + d) % Z, z * 2 + core) for d in range(1, Z)]
    for p in partners:
        greet(p)

    @pl.when(c != z)
    def _():
        greet((z, z * 2 + core))

    xs[...] = x_ref[...] * jnp.bfloat16(SCALE)
    pl.semaphore_wait(barrier, len(partners) + (c != z).astype(jnp.int32))

    started = []

    def remote(src, dst, ss, rs, dev):
        return pltpu.make_async_remote_copy(
            src_ref=src, dst_ref=dst, send_sem=ss, recv_sem=rs, device_id=dev, device_id_type=MESH
        )

    def go(copy):
        copy.start()
        started.append(copy)

    def scatter(d):
        to = (c + d) % Z
        rows = pl.ds(pl.multiple_of(to * 16, 16), 16)
        r = need_slot((z - c) % Z)
        return remote(xs.at[rows], xg.at[core, r, rows], sc_s.at[d], sc_r.at[r], (c, to * 2 + core))

    for d in range(1, Z):
        go(scatter(d))

    @pl.when(c != z)
    def _():
        scatter(0).start()

    mine = pl.ds(pl.multiple_of(c * 16, 16), 16)

    @pl.when(c == z)
    def _():
        xg[core, Z - 1, mine] = xs[mine]

    def scattered(r):
        ref = xg.at[core, r, mine]
        remote(ref, ref, sc_s.at[0], sc_r.at[r], other).wait_recv()

    def bundle(which, n, at, rows):
        first, count = CHUNKS[n]
        return xg.at[which, pl.ds(first, count), pl.ds(pl.multiple_of(at * rows, 16), rows)]

    def x_first(n):
        first, count = CHUNKS[n]
        for r in range(first, first + count):
            if r == Z - 1:
                @pl.when(c != z)
                def _():
                    scattered(r)
            else:
                scattered(r)
        ref = bundle(core, n, c, 16)
        for d in range(1, S):
            go(remote(ref, ref, xy_s.at[n, d - 1], xy_r.at[n, d - 1], y_at(d)))

    def x_second(n):
        for d in range(1, S):
            ref = bundle(core, n, x * S + (y - d) % S, 16)
            remote(ref, ref, xy_s.at[n, d - 1], xy_r.at[n, d - 1], y_at(d)).wait_recv()
        ref = bundle(core, n, x, 64)
        for d in range(1, S):
            go(remote(ref, ref, xx_s.at[n, d - 1], xx_r.at[n, d - 1], x_at(d)))
        go(remote(ref, ref, xc_s.at[n, 0], xc_r.at[n, 0], other))

    def x_third(n):
        for d in range(1, S):
            ref = bundle(core, n, (x - d) % S, 64)
            remote(ref, ref, xx_s.at[n, d - 1], xx_r.at[n, d - 1], x_at(d)).wait_recv()
            go(remote(ref, ref, xc_s.at[n, d], xc_r.at[n, d], other))

    def x_last(n):
        for d in range(S):
            ref = bundle(1 - core, n, (x - d) % S, 64)
            remote(ref, ref, xc_s.at[n, d], xc_r.at[n, d], other).wait_recv()

    def sends(way, h):
        return Z // 2 if way == h else Z // 2 - 1

    def product(r, h, i):
        total = jnp.dot(xg[0, r], w_ref[i, 0:256, lanes(h)], preferred_element_type=jnp.float32)
        return total + jnp.dot(xg[1, r], w_ref[i, 256:512, lanes(h)], preferred_element_type=jnp.float32)

    def hop(way, h, j, i):
        return remote(
            ring.at[h, way, j, i], ring.at[h, way, j + 1, i],
            p_s.at[h, way, j, i], p_r.at[h, way, j, i], z_at(1 - 2 * way),
        )

    def arrived(way, h, j, i):
        ref = ring.at[h, way, j, i]
        remote(ref, ref, p_s.at[h, way, j - 1, i], p_r.at[h, way, j - 1, i], z_at(1 - 2 * way)).wait_recv()

    def compute(h, j):
        ways = [way for way in range(2) if j < sends(way, h)]
        slots = [need_slot((sends(0, h) - j) % Z), need_slot((j - sends(1, h)) % Z)]
        first = ways[0]

        @pl.loop(0, 3 * len(ways))
        def _(q):
            way, i = first + q // 3, q % 3
            part[way, i] = product((1 - way) * slots[0] + way * slots[1], h, i)

    def forward(h, j):
        ways = [way for way in range(2) if j < sends(way, h)]
        first, count = ways[0], len(ways)

        @pl.loop(0, 3 * count)
        def _(q):
            way, i = first + q % count, q // count
            if j == 0:
                ring[h, way, j, i] = coded(part[way, i])
            else:
                arrived(way, h, j, i)
                ring[h, way, j, i] = coded(plain(ring[h, way, j, i]) + part[way, i])
            hop(way, h, j, i).start()

    def project(h):
        @pl.loop(0, 3)
        def _(i):
            part[0, i] = product(Z - 1, h, i)

    def settle(h):
        @pl.loop(0, 3)
        def _(i):
            for way in range(2):
                arrived(way, h, sends(way, h), i)
            total = part[0, i] + plain(ring[h, 0, sends(0, h), i]) + plain(ring[h, 1, sends(1, h), i])
            acc[i] = total * (1.0 / SCALE)

    def halo_copy(h):
        return remote(pad.at[h, :, pl.ds(TOK, 8)], halo.at[h], h_s.at[h], h_r.at[h], z_at(1))

    def part1(h):
        for i in range(3):
            pad[h, i, 8:, :] = acc[i]
        go(halo_copy(h))

    def lanes(h):
        return pl.ds(LANE * h, LANE)

    def state_copy(h, d, src, to):
        return remote(est.at[h, src], est.at[h, src], e_s.at[h, d - 1], e_r.at[h, d - 1], to)

    def part2(h):
        halo_copy(h).wait_recv()
        first = (z > 0).astype(jnp.float32)
        mixed = []
        for i in range(3):
            pad[h, i, 0:8, :] = halo[h, i] * first
            total = jnp.zeros((TOK, LANE), jnp.float32)
            for j in range(TAPS):
                total += sf_ref[i, pl.ds(j, 1), lanes(h)] * pad[h, i, 8 - j : 8 - j + TOK, :]
            mixed.append(total)
        query[h] = mixed[0]
        drive[h] = mixed[1] * mixed[2]
        r = rates_ref[:, lanes(h)]
        f8 = jnp.exp(-8.0 * r)
        steps = [jnp.broadcast_to(f8[m : m + 1, :], (8, LANE)) for m in range(MODES)]

        def one(g, states):
            d = drive[h, pl.ds(pl.multiple_of(g * 8, 8), 8), :]
            return tuple(s * f + d for s, f in zip(states, steps))

        states = lax.fori_loop(0, TOK // 8, one, tuple(jnp.zeros((8, LANE), jnp.float32) for _ in range(MODES)))
        left = 7.0 - lax.broadcasted_iota(jnp.int32, (8, LANE), 0).astype(jnp.float32)
        for m in range(MODES):
            weight = jnp.exp(-r[m : m + 1, :] * left)
            est[h, z, pl.ds(m, 1), :] = jnp.sum(states[m] * weight, axis=0, keepdims=True)
        for d in range(1, Z):
            go(state_copy(h, d, z, z_at(d)))

    def part3(h):
        for d in range(1, Z):
            state_copy(h, d, (z - d) % Z, z_at(d)).wait_recv()
        r = rates_ref[:, lanes(h)]
        block = jnp.exp(-float(TOK) * r)
        entering = jnp.zeros((MODES, LANE), jnp.float32)
        for s in range(Z - 1):
            entering = jnp.where(s < z, entering * block + est[h, s], entering)
        factor = jnp.exp(-r)
        scaled = res_ref[:, lanes(h)] * jnp.sqrt(1.0 - jnp.exp(-2.0 * r))
        fa, fb, sa, sb = factor[:8], factor[8:], scaled[:8], scaled[8:]

        def one(g, state):
            a, b = state
            base = pl.multiple_of(g * 8, 8)
            for t in range(8):
                d = drive[h, pl.ds(base + t, 1), :]
                a = a * fa + d
                b = b * fb + d
                ysum[pl.ds(pl.multiple_of((base + t) * 8, 8), 8), :] = a * sa + b * sb
            return a, b

        lax.fori_loop(0, TOK // 8, one, (entering[:8], entering[8:]))
        total = ysum[pl.ds(0, TOK, stride=8), :]
        for i in range(1, 8):
            total += ysum[pl.ds(i, TOK, stride=8), :]
        gated = query[h] * (total + skip_ref[:, lanes(h)] * drive[h])
        out_ref[:, lanes(h)] = gated.astype(jnp.bfloat16)

    for n in range(len(CHUNKS)):
        x_first(n)
    for n in range(len(CHUNKS)):
        x_second(n)
    ready = {first // 2: n for n, (first, count) in enumerate(CHUNKS)}
    for j in range(Z // 2):
        if j in ready:
            x_third(ready[j])
            x_last(ready[j])
        compute(0, j)
        forward(0, j)
    compute(1, 0)
    forward(1, 0)
    project(0)
    settle(0)
    part1(0)
    for j in range(1, Z // 2):
        compute(1, j)
        forward(1, j)
        if j == 2:
            part2(0)
        if j == 4:
            part3(0)
    project(1)
    settle(1)
    part1(1)
    part2(1)
    part3(1)
    for copy in started:
        copy.wait_send()

    @pl.when(c != z)
    def _():
        scatter(0).wait_send()

    for h in range(2):
        for way in range(2):

            @pl.loop(0, 3 * sends(way, h))
            def _(q):
                hop(way, h, q // 3, q % 3).wait_send()


def per_device(inputs, w_in, short_filter, rates, residues, skip):
    vmem = pl.BlockSpec(memory_space=pltpu.VMEM)
    dma = pltpu.SemaphoreType.DMA
    f32, bf16 = jnp.float32, jnp.bfloat16
    n = len(CHUNKS)
    return pl.pallas_call(
        kernel,
        out_shape=jax.ShapeDtypeStruct(inputs.shape, jnp.bfloat16),
        in_specs=[vmem] * 6,
        out_specs=vmem,
        scratch_shapes=[
            pltpu.VMEM((TOK, 256), bf16),
            pltpu.VMEM((2, Z, TOK, 256), bf16),
            pltpu.VMEM((2, 2, Z // 2 + 1, 3, TOK, LANE), bf16),
            pltpu.VMEM((2, 3, TOK, LANE), f32),
            pltpu.VMEM((3, TOK, LANE), f32),
            pltpu.VMEM((2, 3, TOK + 8, LANE), f32),
            pltpu.VMEM((2, 3, 8, LANE), f32),
            pltpu.VMEM((2, TOK, LANE), f32),
            pltpu.VMEM((2, TOK, LANE), f32),
            pltpu.VMEM((2, Z, MODES, LANE), f32),
            pltpu.VMEM((TOK * 8, LANE), f32),
            dma((Z,)), dma((Z,)),
            dma((n, S - 1)), dma((n, S - 1)), dma((n, S - 1)), dma((n, S - 1)), dma((n, S)), dma((n, S)),
            dma((2, 2, Z // 2, 3)), dma((2, 2, Z // 2, 3)), dma((2,)), dma((2,)),
            dma((2, Z - 1)), dma((2, Z - 1)),
        ],
        compiler_params=pltpu.CompilerParams(
            collective_id=0, has_side_effects=True, vmem_limit_bytes=48 * 2**20
        ),
    )(inputs, w_in, short_filter, rates, residues, skip.reshape(1, -1))


def solution(mesh):
    in_specs = (
        P("seq", "ch"),
        P(None, "seq", "ch"),
        P(None, None, "ch"),
        P(None, "ch"),
        P(None, "ch"),
        P("ch"),
    )
    return jax.shard_map(
        per_device, mesh=mesh, in_specs=in_specs, out_specs=P("seq", "ch"), check_vma=False
    )
```

```python
import functools

import jax
import jax.numpy as jnp
from jax import lax
from jax.experimental import pallas as pl
from jax.experimental.pallas import tpu as pltpu
from jax.sharding import PartitionSpec as P

MESH = pl.DeviceIdType.MESH
Z = 16
S = 4
TOK = 256
LANE = 128
MODES = 16
TAPS = 3


CHUNKS = ((0, 3), (3, 2), (5, 4), (9, 4), (13, 3))
SCALE = 2.0**16


def need_slot(tau):
    ahead = (tau - 1) % Z + 1
    late = (ahead - 1) // (Z // 2)
    return (1 - late) * (Z - 2 * ahead) + late * (2 * ahead - Z - 1)


def need_tau(r):
    return Z // 2 - r // 2 if r % 2 == 0 else (r + Z + 1) // 2


def coded(total):
    return (total * jnp.abs(total) * (total * total)).astype(jnp.bfloat16)


def plain(sent):
    fourth = sent.astype(jnp.float32)
    root = lax.rsqrt(jnp.maximum(jnp.abs(fourth), 1e-37))
    return fourth * root * root * lax.rsqrt(root)


def kernel(
    x_hbm, w_hbm, sf_hbm, rates_hbm, res_hbm, skip_hbm, out_ref,
    x_ref, w_ref, sf_ref, rates_ref, res_ref, skip_ref,
    xs, xp, xg, ring, part, acc, pad, halo, query, drive, est, states_in, ysum,
    in_s, p1_s, p1_r, p2_s, p2_r, xd_s, xd_r, xy_s, xy_r, xx_s, xx_r, xc_s, xc_r, p_s, p_r, h_s, h_r, e_s, e_r,
):
    loads = [
        pltpu.make_async_copy(a, b, in_s.at[n])
        for n, (a, b) in enumerate(
            [(x_hbm, x_ref), (w_hbm, w_ref), (sf_hbm, sf_ref), (rates_hbm, rates_ref), (res_hbm, res_ref), (skip_hbm, skip_ref)]
        )
    ]
    for load in loads:
        load.start()
    z = lax.axis_index("seq")
    ch = lax.axis_index("ch")
    core = ch % 2
    y = (ch // 2) % S
    x = ch // (2 * S)
    c = ch // 2

    def z_at(d):
        return ((z + d) % Z, ch)

    def c_at(d):
        return (z, ((c + d) % Z) * 2 + core)

    def y_at(d):
        return (z, (x * S + (y + d) % S) * 2 + core)

    def x_at(d):
        return (z, (((x + d) % S) * S + y) * 2 + core)

    other = (z, c * 2 + 1 - core)
    barrier = pltpu.get_barrier_semaphore()
    partners = [z_at(d) for d in range(1, Z)] + [c_at(d) for d in range(1, Z)] + [other]
    for p in partners:
        pl.semaphore_signal(barrier, inc=1, device_id=p, device_id_type=MESH)
    loads[0].wait()
    xs[...] = x_ref[...] * jnp.bfloat16(SCALE)
    pl.semaphore_wait(barrier, len(partners))

    started = []

    def remote(src, dst, ss, rs, dev):
        return pltpu.make_async_remote_copy(
            src_ref=src, dst_ref=dst, send_sem=ss, recv_sem=rs, device_id=dev, device_id_type=MESH
        )

    def go(copy):
        copy.start()
        started.append(copy)

    def rows16(at):
        return pl.ds(pl.multiple_of(at * 16, 16), 16)

    mine = rows16(c)

    for d in range(1, Z):
        go(remote(xs.at[rows16((c + d) % Z)], xp.at[c], p1_s.at[d - 1], p1_r.at[d - 1], c_at(d)))
    xp[c] = xs[mine]
    for d in range(1, Z):
        ref = xp.at[(c - d) % Z]
        remote(ref, ref, p1_s.at[d - 1], p1_r.at[d - 1], c_at(d)).wait_recv()
    for r in range(Z - 1):
        tau = need_tau(r)
        go(remote(xp.at[(z - tau) % Z], xg.at[core, r, mine], p2_s.at[r], p2_r.at[r], z_at(-tau)))
    xg[core, Z - 1, mine] = xp[z]

    def scattered(n):
        first, count = CHUNKS[n]
        for r in range(first, min(first + count, Z - 1)):
            ref = xg.at[core, r, mine]
            remote(ref, ref, p2_s.at[r], p2_r.at[r], other).wait_recv()

    def bundle(which, n, at, rows):
        first, count = CHUNKS[n]
        return xg.at[which, pl.ds(first, count), pl.ds(pl.multiple_of(at * rows, 16), rows)]

    def direct(n):
        scattered(n)
        ref = bundle(core, n, c, 16)
        for d in range(1, Z):
            go(remote(ref, ref, xd_s.at[d - 1], xd_r.at[d - 1], c_at(d)))

    def whole(which, n):
        return xg.at[which, pl.ds(*CHUNKS[n])]

    def direct_pass(n):
        for d in range(1, Z):
            ref = bundle(core, n, (c - d) % Z, 16)
            remote(ref, ref, xd_s.at[d - 1], xd_r.at[d - 1], c_at(d)).wait_recv()
        ref = whole(core, n)
        go(remote(ref, ref, xc_s.at[n, 0], xc_r.at[n, 0], other))

    def direct_last(n):
        ref = whole(1 - core, n)
        remote(ref, ref, xc_s.at[n, 0], xc_r.at[n, 0], other).wait_recv()

    def x_first(n):
        scattered(n)
        ref = bundle(core, n, c, 16)
        for d in range(1, S):
            go(remote(ref, ref, xy_s.at[n, d - 1], xy_r.at[n, d - 1], y_at(d)))

    def x_second(n):
        for d in range(1, S):
            ref = bundle(core, n, x * S + (y - d) % S, 16)
            remote(ref, ref, xy_s.at[n, d - 1], xy_r.at[n, d - 1], y_at(d)).wait_recv()
        ref = bundle(core, n, x, 64)
        for d in range(1, S):
            go(remote(ref, ref, xx_s.at[n, d - 1], xx_r.at[n, d - 1], x_at(d)))
        go(remote(ref, ref, xc_s.at[n, 0], xc_r.at[n, 0], other))

    def x_third(n):
        for d in range(1, S):
            ref = bundle(core, n, (x - d) % S, 64)
            remote(ref, ref, xx_s.at[n, d - 1], xx_r.at[n, d - 1], x_at(d)).wait_recv()
            go(remote(ref, ref, xc_s.at[n, d], xc_r.at[n, d], other))

    def x_last(n):
        for d in range(S):
            ref = bundle(1 - core, n, (x - d) % S, 64)
            remote(ref, ref, xc_s.at[n, d], xc_r.at[n, d], other).wait_recv()

    def lanes(h):
        return pl.ds(LANE * h, LANE)

    def long_way(h, i):
        return h + (1 - 2 * h) * (i // 2)

    def product(r, h, i):
        k = (i + 1) % 3
        total = jnp.dot(xg[0, r], w_ref[k, 0:256, lanes(h)], preferred_element_type=jnp.float32)
        return total + jnp.dot(xg[1, r], w_ref[k, 256:512, lanes(h)], preferred_element_type=jnp.float32)

    def hop(way, h, j, i):
        return remote(
            ring.at[h, way, j, i], ring.at[h, way, j + 1, i],
            p_s.at[h, way, j, i], p_r.at[h, way, j, i], z_at(1 - 2 * way),
        )

    def arrived(way, h, j, i):
        ref = ring.at[h, way, j, i]
        remote(ref, ref, p_s.at[h, way, j - 1, i], p_r.at[h, way, j - 1, i], z_at(1 - 2 * way)).wait_recv()

    def each(h, j, body):
        half = Z // 2
        last = j == half - 1

        @pl.loop(0, 3 if last else 6)
        def _(q):
            i = q if last else q // 2
            up = 1 - long_way(h, i)
            way = 1 - up if last else q % 2
            ups = up * need_slot(half - j) + (1 - up) * need_slot(half - 1 - j)
            downs = up * need_slot(half + 1 + j) + (1 - up) * need_slot(half + j)
            body(way, i, (1 - way) * ups + way * downs)

    def launch(h):
        def body(way, i, r):
            ring[h, way, 0, i] = coded(product(r, h, i))
            hop(way, h, 0, i).start()

        each(h, 0, body)

    def compute(h, j):
        def body(way, i, r):
            part[way, i] = product(r, h, i)

        each(h, j, body)

    def forward(h, j):
        def body(way, i, r):
            arrived(way, h, j, i)
            ring[h, way, j, i] = coded(plain(ring[h, way, j, i]) + part[way, i])
            hop(way, h, j, i).start()

        each(h, j, body)

    def project(h):
        @pl.loop(0, 3)
        def _(i):
            acc[i] = product(Z - 1, h, i)

    def settle(h, first, count):
        @pl.loop(first, first + count)
        def _(i):
            ends = [Z // 2 - long_way(h, i), Z // 2 - 1 + long_way(h, i)]
            for way in range(2):
                arrived(way, h, ends[way], i)
            total = acc[i] + plain(ring[h, 0, ends[0], i]) + plain(ring[h, 1, ends[1], i])
            pad[h, i, 8:, :] = total * (1.0 / SCALE)

    def halo_copy(h, n):
        which = pl.ds(0, 2) if n == 0 else pl.ds(2, 1)
        return remote(pad.at[h, which, pl.ds(TOK, 8)], halo.at[h, which], h_s.at[h, n], h_r.at[h, n], z_at(1))

    def part1(h):
        settle(h, 0, 2)
        go(halo_copy(h, 0))
        settle(h, 2, 1)
        go(halo_copy(h, 1))

    def state_copy(h, d, src, to):
        return remote(est.at[h, src], est.at[h, src], e_s.at[h, d - 1], e_r.at[h, d - 1], to)

    def mix(h, i):
        pad[h, i, 0:8, :] = halo[h, i] * (z > 0).astype(jnp.float32)
        total = jnp.zeros((TOK, LANE), jnp.float32)
        for j in range(TAPS):
            total += sf_ref[(i + 1) % 3, pl.ds(j, 1), lanes(h)] * pad[h, i, 8 - j : 8 - j + TOK, :]
        return total

    def part2(h):
        halo_copy(h, 0).wait_recv()
        drive[h] = mix(h, 0) * mix(h, 1)
        r = rates_ref[:, lanes(h)]
        f8 = jnp.exp(-8.0 * r)
        steps = [jnp.broadcast_to(f8[m : m + 1, :], (8, LANE)) for m in range(MODES)]

        def one(g, states):
            d = drive[h, pl.ds(pl.multiple_of(g * 8, 8), 8), :]
            return tuple(s * f + d for s, f in zip(states, steps))

        states = lax.fori_loop(0, TOK // 8, one, tuple(jnp.zeros((8, LANE), jnp.float32) for _ in range(MODES)))
        left = 7.0 - lax.broadcasted_iota(jnp.int32, (8, LANE), 0).astype(jnp.float32)
        for m in range(MODES):
            weight = jnp.exp(-r[m : m + 1, :] * left)
            states_in[pl.ds(m, 1), :] = jnp.sum(states[m] * weight, axis=0, keepdims=True)
        end = states_in[...]
        est[h, z] = (end * jnp.abs(end)).astype(jnp.bfloat16)
        for d in range(1, Z):
            go(state_copy(h, d, z, z_at(d)))
        halo_copy(h, 1).wait_recv()
        query[h] = mix(h, 2)

    def part3(h):
        for d in range(1, Z):
            state_copy(h, d, (z - d) % Z, z_at(d)).wait_recv()
        r = rates_ref[:, lanes(h)]
        block = jnp.exp(-float(TOK) * r)
        entering = jnp.zeros((MODES, LANE), jnp.float32)
        for s in range(Z - 1):
            square = est[h, s].astype(jnp.float32)
            end = square * lax.rsqrt(jnp.maximum(jnp.abs(square), 1e-37))
            entering = jnp.where(s < z, entering * block + end, entering)
        factor = jnp.exp(-r)
        scaled = res_ref[:, lanes(h)] * jnp.sqrt(1.0 - jnp.exp(-2.0 * r))
        fa, fb, sa, sb = factor[:8], factor[8:], scaled[:8], scaled[8:]

        def one(g, state):
            a, b = state
            base = pl.multiple_of(g * 8, 8)
            for t in range(8):
                d = drive[h, pl.ds(base + t, 1), :]
                a = a * fa + d
                b = b * fb + d
                ysum[pl.ds(pl.multiple_of((base + t) * 8, 8), 8), :] = a * sa + b * sb
            return a, b

        lax.fori_loop(0, TOK // 8, one, (entering[:8], entering[8:]))
        total = ysum[pl.ds(0, TOK, stride=8), :]
        for i in range(1, 8):
            total += ysum[pl.ds(i, TOK, stride=8), :]
        gated = query[h] * (total + skip_ref[:, lanes(h)] * drive[h])
        out_ref[:, lanes(h)] = gated.astype(jnp.bfloat16)

    direct(0)
    for load in loads[1:]:
        load.wait()
    x_first(1)
    direct_pass(0)
    for n in range(2, len(CHUNKS)):
        x_first(n)
    x_second(1)
    x_second(2)
    direct_last(0)
    launch(0)
    x_second(3)
    x_second(4)
    ready = {1: 1, 2: 2, 4: 3, 6: 4}
    for j in range(1, Z // 2):
        if j in ready:
            x_third(ready[j])
            x_last(ready[j])
        compute(0, j)
        forward(0, j)
    launch(1)
    project(0)
    part1(0)
    project(1)
    for j in range(1, Z // 2):
        compute(1, j)
        forward(1, j)
        if j == 2:
            part2(0)
        if j == 4:
            part3(0)
    part1(1)
    part2(1)
    part3(1)
    for copy in started:
        copy.wait_send()
    for h in range(2):
        for j in range(Z // 2):

            def drained(way, i, r):
                hop(way, h, j, i).wait_send()

            each(h, j, drained)


def per_device(inputs, w_in, short_filter, rates, residues, skip):
    dma = pltpu.SemaphoreType.DMA
    f32, bf16 = jnp.float32, jnp.bfloat16
    n = len(CHUNKS)
    args = (inputs, w_in, short_filter, rates, residues, skip.reshape(1, -1))
    return pl.pallas_call(
        kernel,
        out_shape=jax.ShapeDtypeStruct(inputs.shape, jnp.bfloat16),
        in_specs=[pl.BlockSpec(memory_space=pl.ANY)] * 6,
        out_specs=pl.BlockSpec(memory_space=pltpu.VMEM),
        scratch_shapes=[pltpu.VMEM(a.shape, a.dtype) for a in args]
        + [
            pltpu.VMEM((TOK, 256), bf16),
            pltpu.VMEM((Z, 16, 256), bf16),
            pltpu.VMEM((2, Z, TOK, 256), bf16),
            pltpu.VMEM((2, 2, Z // 2 + 1, 3, TOK, LANE), bf16),
            pltpu.VMEM((2, 3, TOK, LANE), f32),
            pltpu.VMEM((3, TOK, LANE), f32),
            pltpu.VMEM((2, 3, TOK + 8, LANE), f32),
            pltpu.VMEM((2, 3, 8, LANE), f32),
            pltpu.VMEM((2, TOK, LANE), f32),
            pltpu.VMEM((2, TOK, LANE), f32),
            pltpu.VMEM((2, Z, MODES, LANE), bf16),
            pltpu.VMEM((MODES, LANE), f32),
            pltpu.VMEM((TOK * 8, LANE), f32),
            dma((6,)),
            dma((Z - 1,)), dma((Z - 1,)), dma((Z - 1,)), dma((Z - 1,)), dma((Z - 1,)), dma((Z - 1,)),
            dma((n, S - 1)), dma((n, S - 1)), dma((n, S - 1)), dma((n, S - 1)), dma((n, S)), dma((n, S)),
            dma((2, 2, Z // 2, 3)), dma((2, 2, Z // 2, 3)), dma((2, 2)), dma((2, 2)),
            dma((2, Z - 1)), dma((2, Z - 1)),
        ],
        compiler_params=pltpu.CompilerParams(
            collective_id=0, has_side_effects=True, vmem_limit_bytes=60 * 2**20
        ),
    )(*args)


def solution(mesh):
    in_specs = (
        P("seq", "ch"),
        P(None, "seq", "ch"),
        P(None, None, "ch"),
        P(None, "ch"),
        P(None, "ch"),
        P("ch"),
    )
    return jax.shard_map(
        per_device, mesh=mesh, in_specs=in_specs, out_specs=P("seq", "ch"), check_vma=False
    )
```

```python
import jax
import jax.numpy as jnp
from jax import lax
from jax.experimental import pallas as pl
from jax.experimental.pallas import tpu as pltpu
from jax.sharding import PartitionSpec as P

MESH = pl.DeviceIdType.MESH
Z = 16
HALF = Z // 2
S = 4
TOK = 256
EXT = TOK + 16
LANE = 128
MODES = 16
TAPS = 3
LAG = 5
CHUNKS = ((0, 3), (3, 2), (5, 4), (9, 4), (13, 3))
DIRECT = 2
QROWS = ((0, 144), (144, 128))
SCALE = 2.0**16


def need_slot(tau):
    ahead = (tau - 1) % Z + 1
    late = (ahead - 1) // HALF
    return (1 - late) * (Z - 2 * ahead) + late * (2 * ahead - Z - 1)


def need_tau(r):
    return HALF - r // 2 if r % 2 == 0 else (r + Z + 1) // 2


def coded(total):
    return (total * jnp.abs(total) * (total * total)).astype(jnp.bfloat16)


def plain(sent):
    fourth = sent.astype(jnp.float32)
    root = lax.rsqrt(jnp.maximum(jnp.abs(fourth), 1e-37))
    return fourth * root * root * lax.rsqrt(root)


def kernel(
    x_hbm, w_hbm, sf_hbm, rates_hbm, res_hbm, skip_hbm, out_ref,
    x_ref, w_ref, sf_ref, rates_ref, res_ref, skip_ref,
    xs, xp, xg, ring, qring, part, qpart, own, qown, pad, qpad, halo, drive, conv, est, ends, ysum,
    in_s, p1_s, p1_r, p2_s, p2_r, xd_s, xd_r, xy_s, xy_r, xx_s, xx_r, xc_s, xc_r,
    a_s, a_r, b_s, b_r, h_s, h_r, e_s, e_r,
):
    loads = [
        pltpu.make_async_copy(a, b, in_s.at[n])
        for n, (a, b) in enumerate(
            [(x_hbm, x_ref), (w_hbm, w_ref), (sf_hbm, sf_ref), (rates_hbm, rates_ref), (res_hbm, res_ref), (skip_hbm, skip_ref)]
        )
    ]
    for load in loads:
        load.start()
    z = lax.axis_index("seq")
    ch = lax.axis_index("ch")
    core = ch % 2
    y = (ch // 2) % S
    x = ch // (2 * S)
    c = ch // 2

    def z_at(d):
        return ((z + d) % Z, ch)

    def c_at(d):
        return (z, ((c + d) % Z) * 2 + core)

    def y_at(d):
        return (z, (x * S + (y + d) % S) * 2 + core)

    def x_at(d):
        return (z, (((x + d) % S) * S + y) * 2 + core)

    other = (z, c * 2 + 1 - core)
    barrier = pltpu.get_barrier_semaphore()
    partners = [z_at(d) for d in range(1, Z)] + [c_at(d) for d in range(1, Z)] + [other]
    for p in partners:
        pl.semaphore_signal(barrier, inc=1, device_id=p, device_id_type=MESH)
    loads[0].wait()
    xs[...] = x_ref[...] * jnp.bfloat16(SCALE)
    pl.semaphore_wait(barrier, len(partners))

    def remote(src, dst, ss, rs, dev):
        return pltpu.make_async_remote_copy(
            src_ref=src, dst_ref=dst, send_sem=ss, recv_sem=rs, device_id=dev, device_id_type=MESH
        )

    def take(ref, sem):
        pltpu.make_async_copy(ref, ref, sem).wait()

    def rows16(at):
        return pl.ds(pl.multiple_of(at * 16, 16), 16)

    mine = rows16(c)
    sent = []

    for d in range(1, Z):
        remote(xs.at[rows16((c + d) % Z)], xp.at[c], p1_s.at[0], p1_r.at[0], c_at(d)).start()
    xp[c] = xs[mine]
    take(xp.at[pl.ds(0, Z - 1)], p1_r.at[0])
    sent.append((xp.at[pl.ds(0, Z - 1)], p1_s.at[0]))

    def counted(n):
        first, count = CHUNKS[n]
        return first, min(first + count, Z - 1)

    def along(n):
        first, end = counted(n)
        for r in range(first, end):
            tau = need_tau(r)
            remote(xp.at[(z - tau) % Z], xg.at[core, r, mine], p2_s.at[n], p2_r.at[n], z_at(-tau)).start()
        sent.append((xp.at[pl.ds(0, end - first)], p2_s.at[n]))

    def scattered(n):
        first, end = counted(n)
        take(xg.at[core, pl.ds(first, end - first), mine], p2_r.at[n])

    def bundle(which, n, at, rows):
        first, count = CHUNKS[n]
        return xg.at[which, pl.ds(first, count), pl.ds(pl.multiple_of(at * rows, 16), rows)]

    def whole(which, n):
        return xg.at[which, pl.ds(*CHUNKS[n])]

    def part_of(n, rows):
        first, count = CHUNKS[n]
        return xg.at[core, pl.ds(first, count), pl.ds(0, rows)]

    def cross(n):
        ref = whole(core, n)
        remote(ref, ref, xc_s.at[n], xc_r.at[n], other).start()
        sent.append((ref, xc_s.at[n]))

    def crossed(n):
        take(whole(1 - core, n), xc_r.at[n])

    def direct(n):
        scattered(n)
        ref = bundle(core, n, c, 16)
        for d in range(1, Z):
            remote(ref, ref, xd_s.at[n], xd_r.at[n], c_at(d)).start()
        sent.append((part_of(n, 16 * (Z - 1)), xd_s.at[n]))

    def direct_pass(n):
        take(part_of(n, 16 * (Z - 1)), xd_r.at[n])
        cross(n)

    def x_first(n):
        scattered(n)
        ref = bundle(core, n, c, 16)
        for d in range(1, S):
            remote(ref, ref, xy_s.at[n - DIRECT], xy_r.at[n - DIRECT], y_at(d)).start()
        sent.append((part_of(n, 16 * (S - 1)), xy_s.at[n - DIRECT]))

    def x_second(n):
        take(part_of(n, 16 * (S - 1)), xy_r.at[n - DIRECT])
        ref = bundle(core, n, x, 64)
        for d in range(1, S):
            remote(ref, ref, xx_s.at[n - DIRECT], xx_r.at[n - DIRECT], x_at(d)).start()
        sent.append((part_of(n, 64 * (S - 1)), xx_s.at[n - DIRECT]))

    def x_third(n):
        take(part_of(n, 64 * (S - 1)), xx_r.at[n - DIRECT])
        cross(n)

    def lanes(h):
        return pl.ds(pl.multiple_of(LANE * h, LANE), LANE)

    def times(h, k, rows, r):
        total = jnp.dot(xg[0, r, rows], w_ref[k, 0:256, lanes(h)], preferred_element_type=jnp.float32)
        return total + jnp.dot(xg[1, r, rows], w_ref[k, 256:512, lanes(h)], preferred_element_type=jnp.float32)

    every, tail = slice(0, TOK), slice(TOK - 16, TOK)

    def chains(j, inner, body):
        last = j == HALF - 1

        @pl.loop(0, (2 if last else 4) * inner)
        def _(q):
            if last:
                h, i = q % 2, q // 2
                way = h
            else:
                way, h, i = q % 2, (q // 2) % 2, q // 4

            def pick(back):
                ups = (1 - h) * need_slot(HALF - j - back) + h * need_slot(HALF - 1 - j - back)
                downs = (1 - h) * need_slot(HALF + 1 + j - back) + h * need_slot(HALF + j - back)
                return (1 - way) * ups + way * downs

            body(way, h, i, pick)

    def a_hop(way, h, j, i):
        return remote(
            ring.at[h, way, j, i], ring.at[h, way, j + 1, i],
            a_s.at[h, way, i], a_r.at[h, way, j, i], z_at(1 - 2 * way),
        )

    def b_hop(way, h, j, p):
        rows = pl.ds(*QROWS[p])
        return remote(
            qring.at[h, way, j, rows], qring.at[h, way, j + 1, rows],
            b_s.at[h, way, p], b_r.at[h, way, j, p], z_at(1 - 2 * way),
        )

    def a_launch():
        def body(way, h, i, pick):
            ring[h, way, 0, i] = coded(times(h, i + 1, every, pick(0)))
            a_hop(way, h, 0, i).start()

        chains(0, 2, body)

    def a_compute(j):
        def body(way, h, i, pick):
            part[h, way, i] = times(h, i + 1, every, pick(0))

        chains(j, 2, body)

    def a_forward(j):
        def body(way, h, i, pick):
            a_hop(way, h, j - 1, i).wait()
            ring[h, way, j, i] = coded(plain(ring[h, way, j, i]) + part[h, way, i])
            a_hop(way, h, j, i).start()

        chains(j, 2, body)

    def b_compute(j):
        def body(way, h, i, pick):
            qpart[h, way, 0:16] = times(h, 0, tail, pick(1))
            qpart[h, way, 16:EXT] = times(h, 0, every, pick(0))

        chains(j, 1, body)

    def b_forward(j):
        def body(way, h, i, pick):
            for p in range(2):
                rows = slice(QROWS[p][0], sum(QROWS[p]))
                if j == 0:
                    qring[h, way, j, rows] = coded(qpart[h, way, rows])
                else:
                    b_hop(way, h, j - 1, p).wait()
                    qring[h, way, j, rows] = coded(plain(qring[h, way, j, rows]) + qpart[h, way, rows])
                b_hop(way, h, j, p).start()

        chains(j, 1, body)

    def a_own():
        @pl.loop(0, 4)
        def _(q):
            own[q // 2, q % 2] = times(q // 2, q % 2 + 1, every, Z - 1)

    def b_own():
        @pl.loop(0, 2)
        def _(h):
            qown[h, 0:16] = times(h, 0, tail, need_slot(-1))
            qown[h, 16:EXT] = times(h, 0, every, Z - 1)

    def halo_copy():
        return remote(pad.at[:, :, pl.ds(TOK, 8)], halo, h_s.at[0], h_r.at[0], z_at(1))

    def a_settle():
        @pl.loop(0, 4)
        def _(q):
            h, i = q // 2, q % 2
            stops = (HALF - h, HALF - 1 + h)
            for way in range(2):
                a_hop(way, h, stops[way] - 1, i).wait()
            total = own[h, i] + plain(ring[h, 0, stops[0], i]) + plain(ring[h, 1, stops[1], i])
            pad[h, i, 8:, :] = total * (1.0 / SCALE)

        halo_copy().start()

    first = (z > 0).astype(jnp.float32)

    def part2(h):
        mixed = []
        for i in range(2):
            pad[h, i, 0:8, :] = halo[h, i] * first
            total = jnp.zeros((TOK, LANE), jnp.float32)
            for j in range(TAPS):
                total += sf_ref[i + 1, pl.ds(j, 1), lanes(h)] * pad[h, i, 8 - j : 8 - j + TOK, :]
            mixed.append(total)
        drive[h] = mixed[0] * mixed[1]
        r = rates_ref[:, lanes(h)]
        f8 = jnp.exp(-8.0 * r)
        steps = [jnp.broadcast_to(f8[m : m + 1, :], (8, LANE)) for m in range(MODES)]

        def one(g, states):
            d = drive[h, pl.ds(pl.multiple_of(g * 8, 8), 8), :]
            return tuple(s * f + d for s, f in zip(states, steps))

        states = lax.fori_loop(0, TOK // 8, one, tuple(jnp.zeros((8, LANE), jnp.float32) for _ in range(MODES)))
        left = 7.0 - lax.broadcasted_iota(jnp.int32, (8, LANE), 0).astype(jnp.float32)
        for m in range(MODES):
            weight = jnp.exp(-r[m : m + 1, :] * left)
            ends[pl.ds(m, 1), :] = jnp.sum(states[m] * weight, axis=0, keepdims=True)
        end = ends[...]
        est[z, h] = (end * jnp.abs(end)).astype(jnp.bfloat16)

    def states_out():
        for d in range(1, Z):
            remote(est.at[z], est.at[z], e_s.at[0], e_r.at[0], z_at(d)).start()
        sent.append((est.at[pl.ds(0, Z - 1)], e_s.at[0]))

    def part3(h):
        r = rates_ref[:, lanes(h)]
        block = jnp.exp(-float(TOK) * r)
        entering = jnp.zeros((MODES, LANE), jnp.float32)
        for s in range(Z - 1):
            square = est[s, h].astype(jnp.float32)
            end = square * lax.rsqrt(jnp.maximum(jnp.abs(square), 1e-37))
            entering = jnp.where(s < z, entering * block + end, entering)
        factor = jnp.exp(-r)
        scaled = res_ref[:, lanes(h)] * jnp.sqrt(1.0 - jnp.exp(-2.0 * r))
        fa, fb, sa, sb = factor[:8], factor[8:], scaled[:8], scaled[8:]

        def one(g, state):
            a, b = state
            base = pl.multiple_of(g * 8, 8)
            for t in range(8):
                d = drive[h, pl.ds(base + t, 1), :]
                a = a * fa + d
                b = b * fb + d
                ysum[pl.ds(pl.multiple_of((base + t) * 8, 8), 8), :] = a * sa + b * sb
            return a, b

        lax.fori_loop(0, TOK // 8, one, (entering[:8], entering[8:]))
        total = ysum[pl.ds(0, TOK, stride=8), :]
        for i in range(1, 8):
            total += ysum[pl.ds(i, TOK, stride=8), :]
        conv[h] = total + skip_ref[:, lanes(h)] * drive[h]

    def finish(h):
        stops = (HALF - h, HALF - 1 + h)
        for p in range(2):
            for way in range(2):
                b_hop(way, h, stops[way] - 1, p).wait()
            rows = slice(QROWS[p][0], sum(QROWS[p]))
            total = qown[h, rows] + plain(qring[h, 0, stops[0], rows]) + plain(qring[h, 1, stops[1], rows])
            qpad[rows] = total * (1.0 / SCALE)
        qpad[0:16] = qpad[0:16] * first
        query = jnp.zeros((TOK, LANE), jnp.float32)
        for j in range(TAPS):
            query += sf_ref[0, pl.ds(j, 1), lanes(h)] * qpad[16 - j : 16 - j + TOK, :]
        out_ref[:, LANE * h : LANE * (h + 1)] = (query * conv[h]).astype(jnp.bfloat16)

    along(0)
    direct(0)
    for n in range(1, len(CHUNKS)):
        along(n)
    xg[core, Z - 1, mine] = xp[z]
    direct(1)
    for load in loads[1:]:
        load.wait()
    direct_pass(0)
    for n in range(DIRECT, len(CHUNKS)):
        x_first(n)
    direct_pass(1)
    crossed(0)
    a_launch()
    for n in range(DIRECT, len(CHUNKS)):
        x_second(n)
    ready = {1: 1, 2: 2, 4: 3, 6: 4}
    for step in range(1, HALF + LAG + 1):
        if step in ready:
            n = ready[step]
            if n >= DIRECT:
                x_third(n)
            crossed(n)
        if step < HALF:
            a_compute(step)
            a_forward(step)
        if step == HALF:
            a_settle()
        if LAG <= step < HALF + LAG:
            b_compute(step - LAG)
            b_forward(step - LAG)
        if step == HALF - 1:
            a_own()
        if step == HALF + 1:
            halo_copy().wait()
            part2(0)
            part2(1)
            states_out()
        if step == HALF + 2:
            b_own()
        if step == HALF + 3:
            take(est.at[pl.ds(0, Z - 1)], e_r.at[0])
            part3(0)
        if step == HALF + 4:
            part3(1)
    finish(0)
    finish(1)
    for ref, sem in sent:
        take(ref, sem)


def per_device(inputs, w_in, short_filter, rates, residues, skip):
    dma = pltpu.SemaphoreType.DMA
    f32, bf16 = jnp.float32, jnp.bfloat16
    n = len(CHUNKS)
    args = (inputs, w_in, short_filter, rates, residues, skip.reshape(1, -1))
    return pl.pallas_call(
        kernel,
        out_shape=jax.ShapeDtypeStruct(inputs.shape, jnp.bfloat16),
        in_specs=[pl.BlockSpec(memory_space=pl.ANY)] * 6,
        out_specs=pl.BlockSpec(memory_space=pltpu.VMEM),
        scratch_shapes=[pltpu.VMEM(a.shape, a.dtype) for a in args]
        + [
            pltpu.VMEM((TOK, 256), bf16),
            pltpu.VMEM((Z, 16, 256), bf16),
            pltpu.VMEM((2, Z, TOK, 256), bf16),
            pltpu.VMEM((2, 2, HALF + 1, 2, TOK, LANE), bf16),
            pltpu.VMEM((2, 2, HALF + 1, EXT, LANE), bf16),
            pltpu.VMEM((2, 2, 2, TOK, LANE), f32),
            pltpu.VMEM((2, 2, EXT, LANE), f32),
            pltpu.VMEM((2, 2, TOK, LANE), f32),
            pltpu.VMEM((2, EXT, LANE), f32),
            pltpu.VMEM((2, 2, TOK + 8, LANE), f32),
            pltpu.VMEM((EXT, LANE), f32),
            pltpu.VMEM((2, 2, 8, LANE), f32),
            pltpu.VMEM((2, TOK, LANE), f32),
            pltpu.VMEM((2, TOK, LANE), f32),
            pltpu.VMEM((Z, 2, MODES, LANE), bf16),
            pltpu.VMEM((MODES, LANE), f32),
            pltpu.VMEM((TOK * 8, LANE), f32),
            dma((6,)), dma((1,)), dma((1,)), dma((n,)), dma((n,)), dma((DIRECT,)), dma((DIRECT,)),
            dma((n - DIRECT,)), dma((n - DIRECT,)), dma((n - DIRECT,)), dma((n - DIRECT,)), dma((n,)), dma((n,)),
            dma((2, 2, 2)), dma((2, 2, HALF, 2)), dma((2, 2, 2)), dma((2, 2, HALF, 2)),
            dma((1,)), dma((1,)), dma((1,)), dma((1,)),
        ],
        compiler_params=pltpu.CompilerParams(
            collective_id=0, has_side_effects=True, vmem_limit_bytes=60 * 2**20
        ),
    )(*args)


def solution(mesh):
    in_specs = (
        P("seq", "ch"),
        P(None, "seq", "ch"),
        P(None, None, "ch"),
        P(None, "ch"),
        P(None, "ch"),
        P("ch"),
    )
    return jax.shard_map(
        per_device, mesh=mesh, in_specs=in_specs, out_specs=P("seq", "ch"), check_vma=False
    )
```

```python
import jax
import jax.numpy as jnp
from jax import lax
from jax.experimental import pallas as pl
from jax.experimental.pallas import tpu as pltpu
from jax.sharding import PartitionSpec as P

MESH = pl.DeviceIdType.MESH
Z = 16
HALF = Z // 2
S = 4
TOK = 256
EXT = TOK + 16
LANE = 128
MODES = 16
TAPS = 3
LAG = 4
CHUNKS = ((0, 1), (1, 2), (3, 2), (5, 2), (7, 2), (9, 4), (13, 3))
QROWS = ((0, 144), (144, 128))
SCALE = 2.0**16


def hops(d, size):
    return min(d % size, -d % size)


PLANE = sorted(
    [(i, j) for i in range(S) for j in range(S) if (i, j) != (0, 0)],
    key=lambda d: -hops(d[0], S) - hops(d[1], S),
)
RING = sorted(range(1, Z), key=lambda d: -hops(d, Z))


def need_slot(tau):
    ahead = (tau - 1) % Z + 1
    late = (ahead - 1) // HALF
    return (1 - late) * (Z - 2 * ahead) + late * (2 * ahead - Z - 1)


def need_tau(r):
    return HALF - r // 2 if r % 2 == 0 else (r + Z + 1) // 2


def coded(total):
    return (total * jnp.abs(total) * (total * total)).astype(jnp.bfloat16)


def plain(sent):
    fourth = sent.astype(jnp.float32)
    root = lax.rsqrt(jnp.maximum(jnp.abs(fourth), 1e-37))
    return fourth * root * root * lax.rsqrt(root)


def kernel(
    x_hbm, w_hbm, sf_hbm, rates_hbm, res_hbm, skip_hbm, out_ref,
    x_ref, w_ref, sf_ref, rates_ref, res_ref, skip_ref,
    xs, xp, xg, ring, qring, part, qpart, own, qown, pad, qpad, halo, drive, conv, est, ends, ysum,
    in_s, p1_s, p1_r, p2_s, p2_r, xd_s, xd_r, xc_s, xc_r,
    a_s, a_r, b_s, b_r, h_s, h_r, e_s, e_r,
):
    loads = [
        pltpu.make_async_copy(a, b, in_s.at[n])
        for n, (a, b) in enumerate(
            [(x_hbm, x_ref), (w_hbm, w_ref), (sf_hbm, sf_ref), (rates_hbm, rates_ref), (res_hbm, res_ref), (skip_hbm, skip_ref)]
        )
    ]
    for load in loads:
        load.start()
    z = lax.axis_index("seq")
    ch = lax.axis_index("ch")
    core = ch % 2
    y = (ch // 2) % S
    x = ch // (2 * S)
    c = ch // 2

    def z_at(d):
        return ((z + d) % Z, ch)

    def chip(d):
        return ((x + d[0]) % S) * S + (y + d[1]) % S

    def c_at(d):
        return (z, chip(d) * 2 + core)

    other = (z, c * 2 + 1 - core)
    barrier = pltpu.get_barrier_semaphore()
    partners = [z_at(d) for d in RING] + [c_at(d) for d in PLANE] + [other]
    for p in partners:
        pl.semaphore_signal(barrier, inc=1, device_id=p, device_id_type=MESH)
    loads[0].wait()
    xs[...] = x_ref[...] * jnp.bfloat16(SCALE)
    pl.semaphore_wait(barrier, len(partners))

    def remote(src, dst, ss, rs, dev):
        return pltpu.make_async_remote_copy(
            src_ref=src, dst_ref=dst, send_sem=ss, recv_sem=rs, device_id=dev, device_id_type=MESH
        )

    def take(ref, sem):
        pltpu.make_async_copy(ref, ref, sem).wait()

    def rows16(at):
        return pl.ds(pl.multiple_of(at * 16, 16), 16)

    mine = rows16(c)
    sent = []

    for d in PLANE:
        remote(xs.at[rows16(chip(d))], xp.at[c], p1_s.at[0], p1_r.at[0], c_at(d)).start()
    xp[c] = xs[mine]
    take(xp.at[pl.ds(0, Z - 1)], p1_r.at[0])
    sent.append((xp.at[pl.ds(0, Z - 1)], p1_s.at[0]))

    def counted(n):
        first, count = CHUNKS[n]
        return first, min(first + count, Z - 1)

    def along(n):
        first, end = counted(n)
        for r in range(first, end):
            tau = need_tau(r)
            remote(xp.at[(z - tau) % Z], xg.at[core, r, mine], p2_s.at[n], p2_r.at[n], z_at(-tau)).start()
        sent.append((xp.at[pl.ds(0, end - first)], p2_s.at[n]))

    def scattered(n):
        first, end = counted(n)
        take(xg.at[core, pl.ds(first, end - first), mine], p2_r.at[n])

    def bundle(which, n, at, rows):
        first, count = CHUNKS[n]
        return xg.at[which, pl.ds(first, count), pl.ds(pl.multiple_of(at * rows, 16), rows)]

    def whole(which, n):
        return xg.at[which, pl.ds(*CHUNKS[n])]

    def part_of(n, rows):
        first, count = CHUNKS[n]
        return xg.at[core, pl.ds(first, count), pl.ds(0, rows)]

    def cross(n):
        ref = whole(core, n)
        remote(ref, ref, xc_s.at[n], xc_r.at[n], other).start()
        sent.append((ref, xc_s.at[n]))

    def crossed(n):
        take(whole(1 - core, n), xc_r.at[n])

    def direct(n):
        scattered(n)
        ref = bundle(core, n, c, 16)
        for d in PLANE:
            remote(ref, ref, xd_s.at[n], xd_r.at[n], c_at(d)).start()
        sent.append((part_of(n, 16 * (Z - 1)), xd_s.at[n]))

    def direct_pass(n):
        take(part_of(n, 16 * (Z - 1)), xd_r.at[n])
        cross(n)

    def lanes(h):
        return pl.ds(pl.multiple_of(LANE * h, LANE), LANE)

    def times(h, k, rows, r):
        total = jnp.dot(xg[0, r, rows], w_ref[k, 0:256, lanes(h)], preferred_element_type=jnp.float32)
        return total + jnp.dot(xg[1, r, rows], w_ref[k, 256:512, lanes(h)], preferred_element_type=jnp.float32)

    every, tail = slice(0, TOK), slice(TOK - 16, TOK)

    def chains(j, inner, body):
        last = j == HALF - 1

        @pl.loop(0, (2 if last else 4) * inner)
        def _(q):
            if last:
                h, i = q % 2, q // 2
                way = h
            else:
                way, h, i = q % 2, (q // 2) % 2, q // 4

            def pick(back):
                ups = (1 - h) * need_slot(HALF - j - back) + h * need_slot(HALF - 1 - j - back)
                downs = (1 - h) * need_slot(HALF + 1 + j - back) + h * need_slot(HALF + j - back)
                return (1 - way) * ups + way * downs

            body(way, h, i, pick)

    def a_hop(way, h, j, i):
        return remote(
            ring.at[h, way, j, i], ring.at[h, way, j + 1, i],
            a_s.at[h, way, i], a_r.at[h, way, j, i], z_at(1 - 2 * way),
        )

    def b_hop(way, h, j, p):
        rows = pl.ds(*QROWS[p])
        return remote(
            qring.at[h, way, j, rows], qring.at[h, way, j + 1, rows],
            b_s.at[h, way, p], b_r.at[h, way, j, p], z_at(1 - 2 * way),
        )

    def a_launch(starts, r):
        for way, h in starts:

            @pl.loop(0, 2)
            def _(i):
                ring[h, way, 0, i] = coded(times(h, i + 1, every, r))
                a_hop(way, h, 0, i).start()

    def a_compute(j):
        def body(way, h, i, pick):
            part[h, way, i] = times(h, i + 1, every, pick(0))

        chains(j, 2, body)

    def a_forward(j):
        def body(way, h, i, pick):
            a_hop(way, h, j - 1, i).wait()
            ring[h, way, j, i] = coded(plain(ring[h, way, j, i]) + part[h, way, i])
            a_hop(way, h, j, i).start()

        chains(j, 2, body)

    def b_compute(j):
        def body(way, h, i, pick):
            qpart[h, way, 0:16] = times(h, 0, tail, pick(1))
            qpart[h, way, 16:EXT] = times(h, 0, every, pick(0))

        chains(j, 1, body)

    def b_forward(j):
        def body(way, h, i, pick):
            for p in range(2):
                rows = slice(QROWS[p][0], sum(QROWS[p]))
                if j == 0:
                    qring[h, way, j, rows] = coded(qpart[h, way, rows])
                else:
                    b_hop(way, h, j - 1, p).wait()
                    qring[h, way, j, rows] = coded(plain(qring[h, way, j, rows]) + qpart[h, way, rows])
                b_hop(way, h, j, p).start()

        chains(j, 1, body)

    def a_own():
        @pl.loop(0, 4)
        def _(q):
            own[q // 2, q % 2] = times(q // 2, q % 2 + 1, every, Z - 1)

    def b_own():
        @pl.loop(0, 2)
        def _(h):
            qown[h, 0:16] = times(h, 0, tail, need_slot(-1))
            qown[h, 16:EXT] = times(h, 0, every, Z - 1)

    def halo_copy():
        return remote(pad.at[:, :, pl.ds(TOK, 8)], halo, h_s.at[0], h_r.at[0], z_at(1))

    def a_settle():
        @pl.loop(0, 4)
        def _(q):
            h, i = q // 2, q % 2
            stops = (HALF - h, HALF - 1 + h)
            for way in range(2):
                a_hop(way, h, stops[way] - 1, i).wait()
            total = own[h, i] + plain(ring[h, 0, stops[0], i]) + plain(ring[h, 1, stops[1], i])
            pad[h, i, 8:, :] = total * (1.0 / SCALE)

        halo_copy().start()

    first = (z > 0).astype(jnp.float32)

    def part2(h):
        mixed = []
        for i in range(2):
            pad[h, i, 0:8, :] = halo[h, i] * first
            total = jnp.zeros((TOK, LANE), jnp.float32)
            for j in range(TAPS):
                total += sf_ref[i + 1, pl.ds(j, 1), lanes(h)] * pad[h, i, 8 - j : 8 - j + TOK, :]
            mixed.append(total)
        drive[h] = mixed[0] * mixed[1]
        r = rates_ref[:, lanes(h)]
        f8 = jnp.exp(-8.0 * r)
        steps = [jnp.broadcast_to(f8[m : m + 1, :], (8, LANE)) for m in range(MODES)]

        def one(g, states):
            d = drive[h, pl.ds(pl.multiple_of(g * 8, 8), 8), :]
            return tuple(s * f + d for s, f in zip(states, steps))

        states = lax.fori_loop(0, TOK // 8, one, tuple(jnp.zeros((8, LANE), jnp.float32) for _ in range(MODES)))
        left = 7.0 - lax.broadcasted_iota(jnp.int32, (8, LANE), 0).astype(jnp.float32)
        for m in range(MODES):
            weight = jnp.exp(-r[m : m + 1, :] * left)
            ends[pl.ds(m, 1), :] = jnp.sum(states[m] * weight, axis=0, keepdims=True)
        end = ends[...]
        est[z, h] = (end * jnp.abs(end)).astype(jnp.bfloat16)

    def states_out():
        for d in RING:
            remote(est.at[z], est.at[z], e_s.at[0], e_r.at[0], z_at(d)).start()
        sent.append((est.at[pl.ds(0, Z - 1)], e_s.at[0]))

    def part3(h):
        r = rates_ref[:, lanes(h)]
        block = jnp.exp(-float(TOK) * r)
        entering = jnp.zeros((MODES, LANE), jnp.float32)
        for s in range(Z - 1):
            square = est[s, h].astype(jnp.float32)
            end = square * lax.rsqrt(jnp.maximum(jnp.abs(square), 1e-37))
            entering = jnp.where(s < z, entering * block + end, entering)
        factor = jnp.exp(-r)
        scaled = res_ref[:, lanes(h)] * jnp.sqrt(1.0 - jnp.exp(-2.0 * r))
        fa, fb, sa, sb = factor[:8], factor[8:], scaled[:8], scaled[8:]

        def one(g, state):
            a, b = state
            base = pl.multiple_of(g * 8, 8)
            for t in range(8):
                d = drive[h, pl.ds(base + t, 1), :]
                a = a * fa + d
                b = b * fb + d
                ysum[pl.ds(pl.multiple_of((base + t) * 8, 8), 8), :] = a * sa + b * sb
            return a, b

        lax.fori_loop(0, TOK // 8, one, (entering[:8], entering[8:]))
        total = ysum[pl.ds(0, TOK, stride=8), :]
        for i in range(1, 8):
            total += ysum[pl.ds(i, TOK, stride=8), :]
        conv[h] = total + skip_ref[:, lanes(h)] * drive[h]

    def finish(h):
        stops = (HALF - h, HALF - 1 + h)
        for p in range(2):
            for way in range(2):
                b_hop(way, h, stops[way] - 1, p).wait()
            rows = slice(QROWS[p][0], sum(QROWS[p]))
            total = qown[h, rows] + plain(qring[h, 0, stops[0], rows]) + plain(qring[h, 1, stops[1], rows])
            qpad[rows] = total * (1.0 / SCALE)
        qpad[0:16] = qpad[0:16] * first
        query = jnp.zeros((TOK, LANE), jnp.float32)
        for j in range(TAPS):
            query += sf_ref[0, pl.ds(j, 1), lanes(h)] * qpad[16 - j : 16 - j + TOK, :]
        out_ref[:, LANE * h : LANE * (h + 1)] = (query * conv[h]).astype(jnp.bfloat16)

    along(0)
    along(1)
    along(2)
    direct(0)
    direct(1)
    along(3)
    along(4)
    along(5)
    along(6)
    xg[core, Z - 1, mine] = xp[z]
    for load in loads[1:]:
        load.wait()
    direct(2)
    direct_pass(0)
    direct_pass(1)
    crossed(0)
    a_launch(((0, 0), (1, 1)), need_slot(HALF))
    direct(3)
    crossed(1)
    a_launch(((1, 0),), need_slot(HALF + 1))
    a_launch(((0, 1),), need_slot(HALF - 1))
    direct(4)
    direct_pass(2)
    direct(5)
    direct(6)
    ready = {1: 2, 2: 3, 3: 4, 4: 5, 6: 6}
    for step in range(1, HALF + LAG + 1):
        if step in ready:
            crossed(ready[step])
        if step < HALF:
            a_compute(step)
            a_forward(step)
        if step + 1 in ready:
            direct_pass(ready[step + 1])
        if step == HALF:
            a_settle()
        if LAG <= step < HALF + LAG:
            b_compute(step - LAG)
            b_forward(step - LAG)
        if step == HALF - 1:
            a_own()
        if step == HALF + 1:
            halo_copy().wait()
            part2(0)
            part2(1)
            states_out()
        if step == HALF + 2:
            b_own()
        if step == HALF + 3:
            take(est.at[pl.ds(0, Z - 1)], e_r.at[0])
            part3(0)
        if step == HALF + 4:
            part3(1)
    finish(0)
    finish(1)
    for ref, sem in sent:
        take(ref, sem)


def per_device(inputs, w_in, short_filter, rates, residues, skip):
    dma = pltpu.SemaphoreType.DMA
    f32, bf16 = jnp.float32, jnp.bfloat16
    n = len(CHUNKS)
    args = (inputs, w_in, short_filter, rates, residues, skip.reshape(1, -1))
    return pl.pallas_call(
        kernel,
        out_shape=jax.ShapeDtypeStruct(inputs.shape, jnp.bfloat16),
        in_specs=[pl.BlockSpec(memory_space=pl.ANY)] * 6,
        out_specs=pl.BlockSpec(memory_space=pltpu.VMEM),
        scratch_shapes=[pltpu.VMEM(a.shape, a.dtype) for a in args]
        + [
            pltpu.VMEM((TOK, 256), bf16),
            pltpu.VMEM((Z, 16, 256), bf16),
            pltpu.VMEM((2, Z, TOK, 256), bf16),
            pltpu.VMEM((2, 2, HALF + 1, 2, TOK, LANE), bf16),
            pltpu.VMEM((2, 2, HALF + 1, EXT, LANE), bf16),
            pltpu.VMEM((2, 2, 2, TOK, LANE), f32),
            pltpu.VMEM((2, 2, EXT, LANE), f32),
            pltpu.VMEM((2, 2, TOK, LANE), f32),
            pltpu.VMEM((2, EXT, LANE), f32),
            pltpu.VMEM((2, 2, TOK + 8, LANE), f32),
            pltpu.VMEM((EXT, LANE), f32),
            pltpu.VMEM((2, 2, 8, LANE), f32),
            pltpu.VMEM((2, TOK, LANE), f32),
            pltpu.VMEM((2, TOK, LANE), f32),
            pltpu.VMEM((Z, 2, MODES, LANE), bf16),
            pltpu.VMEM((MODES, LANE), f32),
            pltpu.VMEM((TOK * 8, LANE), f32),
            dma((6,)), dma((1,)), dma((1,)), dma((n,)), dma((n,)), dma((n,)), dma((n,)),
            dma((n,)), dma((n,)),
            dma((2, 2, 2)), dma((2, 2, HALF, 2)), dma((2, 2, 2)), dma((2, 2, HALF, 2)),
            dma((1,)), dma((1,)), dma((1,)), dma((1,)),
        ],
        compiler_params=pltpu.CompilerParams(
            collective_id=0, has_side_effects=True, vmem_limit_bytes=60 * 2**20
        ),
    )(*args)


def solution(mesh):
    in_specs = (
        P("seq", "ch"),
        P(None, "seq", "ch"),
        P(None, None, "ch"),
        P(None, "ch"),
        P(None, "ch"),
        P("ch"),
    )
    return jax.shard_map(
        per_device, mesh=mesh, in_specs=in_specs, out_specs=P("seq", "ch"), check_vma=False
    )
```

```python
import jax
import jax.numpy as jnp
from jax import lax
from jax.experimental import pallas as pl
from jax.experimental.pallas import tpu as pltpu
from jax.sharding import PartitionSpec as P

MESH = pl.DeviceIdType.MESH
Z = 16
HALF = Z // 2
S = 4
TOK = 256
EXT = TOK + 16
LANE = 128
MODES = 16
TAPS = 3
LAG = 3
CHUNKS = ((0, 1), (1, 2), (3, 2), (5, 2), (7, 2), (9, 4), (13, 3))
QROWS = ((0, 144), (144, 128))
SCALE = 2.0**16


def hops(d, size):
    return min(d % size, -d % size)


PLANE = sorted(
    [(i, j) for i in range(S) for j in range(S) if (i, j) != (0, 0)],
    key=lambda d: -hops(d[0], S) - hops(d[1], S),
)
RING = sorted(range(1, Z), key=lambda d: -hops(d, Z))


def need_slot(tau):
    ahead = (tau - 1) % Z + 1
    late = (ahead - 1) // HALF
    return (1 - late) * (Z - 2 * ahead) + late * (2 * ahead - Z - 1)


def need_tau(r):
    return HALF - r // 2 if r % 2 == 0 else (r + Z + 1) // 2


def coded(total):
    return (total * jnp.abs(total) * (total * total)).astype(jnp.bfloat16)


def plain(sent):
    fourth = sent.astype(jnp.float32)
    root = lax.rsqrt(jnp.maximum(jnp.abs(fourth), 1e-37))
    return fourth * root * root * lax.rsqrt(root)


def kernel(
    x_hbm, w_hbm, sf_hbm, rates_hbm, res_hbm, skip_hbm, out_ref,
    x_ref, w_ref, sf_ref, rates_ref, res_ref, skip_ref,
    xs, xp, xg, ring, qring, part, qpart, own, qown, pad, qpad, halo, drive, conv, est, ends, ysum,
    in_s, p1_s, p1_r, p2_s, p2_r, xd_s, xd_r, xc_s, xc_r,
    a_s, a_r, b_s, b_r, h_s, h_r, e_s, e_r,
):
    loads = [
        pltpu.make_async_copy(a, b, in_s.at[n])
        for n, (a, b) in enumerate(
            [(x_hbm, x_ref), (w_hbm, w_ref), (sf_hbm, sf_ref), (rates_hbm, rates_ref), (res_hbm, res_ref), (skip_hbm, skip_ref)]
        )
    ]
    for load in loads:
        load.start()
    z = lax.axis_index("seq")
    ch = lax.axis_index("ch")
    core = ch % 2
    y = (ch // 2) % S
    x = ch // (2 * S)
    c = ch // 2

    def z_at(d):
        return ((z + d) % Z, ch)

    def chip(d):
        return ((x + d[0]) % S) * S + (y + d[1]) % S

    def c_at(d):
        return (z, chip(d) * 2 + core)

    other = (z, c * 2 + 1 - core)
    barrier = pltpu.get_barrier_semaphore()
    partners = [z_at(d) for d in RING] + [c_at(d) for d in PLANE] + [other]
    for p in partners:
        pl.semaphore_signal(barrier, inc=1, device_id=p, device_id_type=MESH)
    loads[0].wait()
    xs[...] = x_ref[...] * jnp.bfloat16(SCALE)
    pl.semaphore_wait(barrier, len(partners))

    def remote(src, dst, ss, rs, dev):
        return pltpu.make_async_remote_copy(
            src_ref=src, dst_ref=dst, send_sem=ss, recv_sem=rs, device_id=dev, device_id_type=MESH
        )

    def take(ref, sem):
        pltpu.make_async_copy(ref, ref, sem).wait()

    def rows16(at):
        return pl.ds(pl.multiple_of(at * 16, 16), 16)

    mine = rows16(c)
    sent = []

    for d in PLANE:
        remote(xs.at[rows16(chip(d))], xp.at[c], p1_s.at[0], p1_r.at[0], c_at(d)).start()
    xp[c] = xs[mine]
    take(xp.at[pl.ds(0, Z - 1)], p1_r.at[0])
    sent.append((xp.at[pl.ds(0, Z - 1)], p1_s.at[0]))

    def counted(n):
        first, count = CHUNKS[n]
        return first, min(first + count, Z - 1)

    def along(n):
        first, end = counted(n)
        for r in range(first, end):
            tau = need_tau(r)
            remote(xp.at[(z - tau) % Z], xg.at[core, r, mine], p2_s.at[n], p2_r.at[n], z_at(-tau)).start()
        sent.append((xp.at[pl.ds(0, end - first)], p2_s.at[n]))

    def scattered(n):
        first, end = counted(n)
        take(xg.at[core, pl.ds(first, end - first), mine], p2_r.at[n])

    def bundle(which, n, at, rows):
        first, count = CHUNKS[n]
        return xg.at[which, pl.ds(first, count), pl.ds(pl.multiple_of(at * rows, 16), rows)]

    def whole(which, n):
        return xg.at[which, pl.ds(*CHUNKS[n])]

    def part_of(n, rows):
        first, count = CHUNKS[n]
        return xg.at[core, pl.ds(first, count), pl.ds(0, rows)]

    def cross(n):
        ref = whole(core, n)
        remote(ref, ref, xc_s.at[n], xc_r.at[n], other).start()
        sent.append((ref, xc_s.at[n]))

    def crossed(n):
        take(whole(1 - core, n), xc_r.at[n])

    def direct(n):
        scattered(n)
        ref = bundle(core, n, c, 16)
        for d in PLANE:
            remote(ref, ref, xd_s.at[n], xd_r.at[n], c_at(d)).start()
        sent.append((part_of(n, 16 * (Z - 1)), xd_s.at[n]))

    def direct_pass(n):
        take(part_of(n, 16 * (Z - 1)), xd_r.at[n])
        cross(n)

    def lanes(h):
        return pl.ds(pl.multiple_of(LANE * h, LANE), LANE)

    def times(h, k, rows, r):
        total = jnp.dot(xg[0, r, rows], w_ref[k, 0:256, lanes(h)], preferred_element_type=jnp.float32)
        return total + jnp.dot(xg[1, r, rows], w_ref[k, 256:512, lanes(h)], preferred_element_type=jnp.float32)

    every, tail = slice(0, TOK), slice(TOK - 16, TOK)

    def chains(j, inner, body):
        last = j == HALF - 1

        @pl.loop(0, (2 if last else 4) * inner)
        def _(q):
            if last:
                h, i = q % 2, q // 2
                way = h
            else:
                way, h, i = q % 2, (q // 2) % 2, q // 4

            def pick(back):
                ups = (1 - h) * need_slot(HALF - j - back) + h * need_slot(HALF - 1 - j - back)
                downs = (1 - h) * need_slot(HALF + 1 + j - back) + h * need_slot(HALF + j - back)
                return (1 - way) * ups + way * downs

            body(way, h, i, pick)

    def a_hop(way, h, j, i):
        return remote(
            ring.at[h, way, j, i], ring.at[h, way, j + 1, i],
            a_s.at[h, way, i], a_r.at[h, way, j, i], z_at(1 - 2 * way),
        )

    def b_hop(way, h, j, p):
        rows = pl.ds(*QROWS[p])
        return remote(
            qring.at[h, way, j, rows], qring.at[h, way, j + 1, rows],
            b_s.at[h, way, p], b_r.at[h, way, j, p], z_at(1 - 2 * way),
        )

    def a_launch(starts, r):
        for way, h in starts:

            @pl.loop(0, 2)
            def _(i):
                ring[h, way, 0, i] = coded(times(h, i + 1, every, r))
                a_hop(way, h, 0, i).start()

    def a_compute(j):
        def body(way, h, i, pick):
            part[h, way, i] = times(h, i + 1, every, pick(0))

        chains(j, 2, body)

    def a_forward(j):
        def body(way, h, i, pick):
            a_hop(way, h, j - 1, i).wait()
            ring[h, way, j, i] = coded(plain(ring[h, way, j, i]) + part[h, way, i])
            a_hop(way, h, j, i).start()

        chains(j, 2, body)

    def b_compute(j):
        def body(way, h, i, pick):
            qpart[h, way, 0:16] = times(h, 0, tail, pick(1))
            qpart[h, way, 16:EXT] = times(h, 0, every, pick(0))

        chains(j, 1, body)

    def b_forward(j):
        def body(way, h, i, pick):
            for p in range(2):
                rows = slice(QROWS[p][0], sum(QROWS[p]))
                if j == 0:
                    qring[h, way, j, rows] = coded(qpart[h, way, rows])
                else:
                    b_hop(way, h, j - 1, p).wait()
                    qring[h, way, j, rows] = coded(plain(qring[h, way, j, rows]) + qpart[h, way, rows])
                b_hop(way, h, j, p).start()

        chains(j, 1, body)

    def a_own():
        @pl.loop(0, 4)
        def _(q):
            own[q // 2, q % 2] = times(q // 2, q % 2 + 1, every, Z - 1)

    def b_own():
        @pl.loop(0, 2)
        def _(h):
            qown[h, 0:16] = times(h, 0, tail, need_slot(-1))
            qown[h, 16:EXT] = times(h, 0, every, Z - 1)

    def halo_copy():
        return remote(pad.at[:, :, pl.ds(TOK, 8)], halo, h_s.at[0], h_r.at[0], z_at(1))

    def a_settle():
        @pl.loop(0, 4)
        def _(q):
            h, i = q // 2, q % 2
            stops = (HALF - h, HALF - 1 + h)
            for way in range(2):
                a_hop(way, h, stops[way] - 1, i).wait()
            total = own[h, i] + plain(ring[h, 0, stops[0], i]) + plain(ring[h, 1, stops[1], i])
            pad[h, i, 8:, :] = total * (1.0 / SCALE)

        halo_copy().start()

    first = (z > 0).astype(jnp.float32)

    def part2(h):
        mixed = []
        for i in range(2):
            pad[h, i, 0:8, :] = halo[h, i] * first
            total = jnp.zeros((TOK, LANE), jnp.float32)
            for j in range(TAPS):
                total += sf_ref[i + 1, pl.ds(j, 1), lanes(h)] * pad[h, i, 8 - j : 8 - j + TOK, :]
            mixed.append(total)
        drive[h] = mixed[0] * mixed[1]
        r = rates_ref[:, lanes(h)]
        f8 = jnp.exp(-8.0 * r)
        steps = [jnp.broadcast_to(f8[m : m + 1, :], (8, LANE)) for m in range(MODES)]

        def one(g, states):
            d = drive[h, pl.ds(pl.multiple_of(g * 8, 8), 8), :]
            return tuple(s * f + d for s, f in zip(states, steps))

        states = lax.fori_loop(0, TOK // 8, one, tuple(jnp.zeros((8, LANE), jnp.float32) for _ in range(MODES)))
        left = 7.0 - lax.broadcasted_iota(jnp.int32, (8, LANE), 0).astype(jnp.float32)
        for m in range(MODES):
            weight = jnp.exp(-r[m : m + 1, :] * left)
            ends[pl.ds(m, 1), :] = jnp.sum(states[m] * weight, axis=0, keepdims=True)
        end = ends[...]
        est[z, h] = (end * jnp.abs(end)).astype(jnp.bfloat16)

    def states_out():
        for d in RING:
            remote(est.at[z], est.at[z], e_s.at[0], e_r.at[0], z_at(d)).start()
        sent.append((est.at[pl.ds(0, Z - 1)], e_s.at[0]))

    def part3(h):
        r = rates_ref[:, lanes(h)]
        block = jnp.exp(-float(TOK) * r)
        entering = jnp.zeros((MODES, LANE), jnp.float32)
        for s in range(Z - 1):
            square = est[s, h].astype(jnp.float32)
            end = square * lax.rsqrt(jnp.maximum(jnp.abs(square), 1e-37))
            entering = jnp.where(s < z, entering * block + end, entering)
        factor = jnp.exp(-r)
        scaled = res_ref[:, lanes(h)] * jnp.sqrt(1.0 - jnp.exp(-2.0 * r))
        fa, fb, sa, sb = factor[:8], factor[8:], scaled[:8], scaled[8:]

        def one(g, state):
            a, b = state
            base = pl.multiple_of(g * 8, 8)
            for t in range(8):
                d = drive[h, pl.ds(base + t, 1), :]
                a = a * fa + d
                b = b * fb + d
                ysum[pl.ds(pl.multiple_of((base + t) * 8, 8), 8), :] = a * sa + b * sb
            return a, b

        lax.fori_loop(0, TOK // 8, one, (entering[:8], entering[8:]))
        total = ysum[pl.ds(0, TOK, stride=8), :]
        for i in range(1, 8):
            total += ysum[pl.ds(i, TOK, stride=8), :]
        conv[h] = total + skip_ref[:, lanes(h)] * drive[h]

    def finish(h):
        stops = (HALF - h, HALF - 1 + h)
        for p in range(2):
            for way in range(2):
                b_hop(way, h, stops[way] - 1, p).wait()
            rows = slice(QROWS[p][0], sum(QROWS[p]))
            total = qown[h, rows] + plain(qring[h, 0, stops[0], rows]) + plain(qring[h, 1, stops[1], rows])
            qpad[rows] = total * (1.0 / SCALE)
        qpad[0:16] = qpad[0:16] * first
        query = jnp.zeros((TOK, LANE), jnp.float32)
        for j in range(TAPS):
            query += sf_ref[0, pl.ds(j, 1), lanes(h)] * qpad[16 - j : 16 - j + TOK, :]
        out_ref[:, LANE * h : LANE * (h + 1)] = (query * conv[h]).astype(jnp.bfloat16)

    along(0)
    along(1)
    along(2)
    direct(0)
    direct(1)
    along(3)
    along(4)
    along(5)
    along(6)
    xg[core, Z - 1, mine] = xp[z]
    for load in loads[1:]:
        load.wait()
    direct(2)
    direct_pass(0)
    direct_pass(1)
    crossed(0)
    a_launch(((0, 0), (1, 1)), need_slot(HALF))
    direct(3)
    crossed(1)
    a_launch(((1, 0),), need_slot(HALF + 1))
    a_launch(((0, 1),), need_slot(HALF - 1))
    direct(4)
    direct_pass(2)
    direct(5)
    direct(6)
    ready = {1: 2, 2: 3, 3: 4, 4: 5, 6: 6}
    for step in range(1, HALF + LAG + 1):
        if step in ready:
            crossed(ready[step])
        if step < HALF:
            a_compute(step)
            a_forward(step)
        if step + 1 in ready:
            direct_pass(ready[step + 1])
        if step == HALF:
            a_settle()
        if LAG <= step < HALF + LAG:
            b_compute(step - LAG)
            b_forward(step - LAG)
        if step == HALF - 1:
            a_own()
        if step == HALF:
            halo_copy().wait()
            part2(0)
            part2(1)
            states_out()
        if step == HALF + 1:
            b_own()
        if step == HALF + 2:
            take(est.at[pl.ds(0, Z - 1)], e_r.at[0])
            part3(0)
        if step == HALF + 3:
            part3(1)
    finish(0)
    finish(1)
    for ref, sem in sent:
        take(ref, sem)


def per_device(inputs, w_in, short_filter, rates, residues, skip):
    dma = pltpu.SemaphoreType.DMA
    f32, bf16 = jnp.float32, jnp.bfloat16
    n = len(CHUNKS)
    args = (inputs, w_in, short_filter, rates, residues, skip.reshape(1, -1))
    return pl.pallas_call(
        kernel,
        out_shape=jax.ShapeDtypeStruct(inputs.shape, jnp.bfloat16),
        in_specs=[pl.BlockSpec(memory_space=pl.ANY)] * 6,
        out_specs=pl.BlockSpec(memory_space=pltpu.VMEM),
        scratch_shapes=[pltpu.VMEM(a.shape, a.dtype) for a in args]
        + [
            pltpu.VMEM((TOK, 256), bf16),
            pltpu.VMEM((Z, 16, 256), bf16),
            pltpu.VMEM((2, Z, TOK, 256), bf16),
            pltpu.VMEM((2, 2, HALF + 1, 2, TOK, LANE), bf16),
            pltpu.VMEM((2, 2, HALF + 1, EXT, LANE), bf16),
            pltpu.VMEM((2, 2, 2, TOK, LANE), f32),
            pltpu.VMEM((2, 2, EXT, LANE), f32),
            pltpu.VMEM((2, 2, TOK, LANE), f32),
            pltpu.VMEM((2, EXT, LANE), f32),
            pltpu.VMEM((2, 2, TOK + 8, LANE), f32),
            pltpu.VMEM((EXT, LANE), f32),
            pltpu.VMEM((2, 2, 8, LANE), f32),
            pltpu.VMEM((2, TOK, LANE), f32),
            pltpu.VMEM((2, TOK, LANE), f32),
            pltpu.VMEM((Z, 2, MODES, LANE), bf16),
            pltpu.VMEM((MODES, LANE), f32),
            pltpu.VMEM((TOK * 8, LANE), f32),
            dma((6,)), dma((1,)), dma((1,)), dma((n,)), dma((n,)), dma((n,)), dma((n,)),
            dma((n,)), dma((n,)),
            dma((2, 2, 2)), dma((2, 2, HALF, 2)), dma((2, 2, 2)), dma((2, 2, HALF, 2)),
            dma((1,)), dma((1,)), dma((1,)), dma((1,)),
        ],
        compiler_params=pltpu.CompilerParams(
            collective_id=0, has_side_effects=True, vmem_limit_bytes=60 * 2**20
        ),
    )(*args)


def solution(mesh):
    in_specs = (
        P("seq", "ch"),
        P(None, "seq", "ch"),
        P(None, None, "ch"),
        P(None, "ch"),
        P(None, "ch"),
        P("ch"),
    )
    return jax.shard_map(
        per_device, mesh=mesh, in_specs=in_specs, out_specs=P("seq", "ch"), check_vma=False
    )
```

```python
import jax
import jax.numpy as jnp
from jax import lax
from jax.experimental import pallas as pl
from jax.experimental.pallas import tpu as pltpu
from jax.sharding import PartitionSpec as P

MESH = pl.DeviceIdType.MESH
Z = 16
HALF = Z // 2
S = 4
TOK = 256
EXT = TOK + 16
LANE = 128
MODES = 16
TAPS = 3
LAG = 3
CHUNKS = ((0, 1), (1, 2), (3, 2), (5, 2), (7, 2), (9, 4), (13, 3))
QROWS = ((0, 144), (144, 128))
SCALE = 2.0**16


def hops(d, size):
    return min(d % size, -d % size)


PLANE = sorted(
    [(i, j) for i in range(S) for j in range(S) if (i, j) != (0, 0)],
    key=lambda d: -hops(d[0], S) - hops(d[1], S),
)
RING = sorted(range(1, Z), key=lambda d: -hops(d, Z))


def need_slot(tau):
    ahead = (tau - 1) % Z + 1
    late = (ahead - 1) // HALF
    return (1 - late) * (Z - 2 * ahead) + late * (2 * ahead - Z - 1)


def need_tau(r):
    return HALF - r // 2 if r % 2 == 0 else (r + Z + 1) // 2


def coded(total):
    return (total * jnp.abs(total) * (total * total)).astype(jnp.bfloat16)


def plain(sent):
    fourth = sent.astype(jnp.float32)
    root = lax.rsqrt(jnp.maximum(jnp.abs(fourth), 1e-37))
    return fourth * root * root * lax.rsqrt(root)


def kernel(
    x_hbm, w_hbm, sf_hbm, rates_hbm, res_hbm, skip_hbm, out_ref,
    x_ref, w_ref, sf_ref, rates_ref, res_ref, skip_ref,
    xs, xp, xg, ring, qring, part, qpart, own, qown, pad, qpad, halo, drive, conv, est, ends, ysum,
    in_s, p1_s, p1_r, p2_s, p2_r, xd_s, xd_r, xc_s, xc_r,
    a_s, a_r, b_s, b_r, h_s, h_r, e_s, e_r,
):
    loads = [
        pltpu.make_async_copy(a, b, in_s.at[n])
        for n, (a, b) in enumerate(
            [(x_hbm, x_ref), (w_hbm, w_ref), (sf_hbm, sf_ref), (rates_hbm, rates_ref), (res_hbm, res_ref), (skip_hbm, skip_ref)]
        )
    ]
    for load in loads:
        load.start()
    z = lax.axis_index("seq")
    ch = lax.axis_index("ch")
    core = ch % 2
    y = (ch // 2) % S
    x = ch // (2 * S)
    c = ch // 2

    def z_at(d):
        return ((z + d) % Z, ch)

    def chip(d):
        return ((x + d[0]) % S) * S + (y + d[1]) % S

    def c_at(d):
        return (z, chip(d) * 2 + core)

    other = (z, c * 2 + 1 - core)
    barrier = pltpu.get_barrier_semaphore()
    partners = [z_at(d) for d in RING] + [c_at(d) for d in PLANE] + [other]
    for p in partners:
        pl.semaphore_signal(barrier, inc=1, device_id=p, device_id_type=MESH)
    loads[0].wait()
    xs[...] = x_ref[...] * jnp.bfloat16(SCALE)
    pl.semaphore_wait(barrier, len(partners))

    def remote(src, dst, ss, rs, dev):
        return pltpu.make_async_remote_copy(
            src_ref=src, dst_ref=dst, send_sem=ss, recv_sem=rs, device_id=dev, device_id_type=MESH
        )

    def take(ref, sem):
        pltpu.make_async_copy(ref, ref, sem).wait()

    def rows16(at):
        return pl.ds(pl.multiple_of(at * 16, 16), 16)

    mine = rows16(c)
    sent = []

    for d in PLANE:
        remote(xs.at[rows16(chip(d))], xp.at[c], p1_s.at[0], p1_r.at[0], c_at(d)).start()
    xp[c] = xs[mine]
    take(xp.at[pl.ds(0, Z - 1)], p1_r.at[0])
    sent.append((xp.at[pl.ds(0, Z - 1)], p1_s.at[0]))

    def counted(n):
        first, count = CHUNKS[n]
        return first, min(first + count, Z - 1)

    def along(n):
        first, end = counted(n)
        for r in range(first, end):
            tau = need_tau(r)
            remote(xp.at[(z - tau) % Z], xg.at[core, r, mine], p2_s.at[n], p2_r.at[n], z_at(-tau)).start()
        sent.append((xp.at[pl.ds(0, end - first)], p2_s.at[n]))

    def scattered(n):
        first, end = counted(n)
        take(xg.at[core, pl.ds(first, end - first), mine], p2_r.at[n])

    def bundle(which, n, at, rows):
        first, count = CHUNKS[n]
        return xg.at[which, pl.ds(first, count), pl.ds(pl.multiple_of(at * rows, 16), rows)]

    def whole(which, n):
        return xg.at[which, pl.ds(*CHUNKS[n])]

    def part_of(n, rows):
        first, count = CHUNKS[n]
        return xg.at[core, pl.ds(first, count), pl.ds(0, rows)]

    def cross(n):
        ref = whole(core, n)
        remote(ref, ref, xc_s.at[n], xc_r.at[n], other).start()
        sent.append((ref, xc_s.at[n]))

    def crossed(n):
        take(whole(1 - core, n), xc_r.at[n])

    def direct(n):
        scattered(n)
        ref = bundle(core, n, c, 16)
        for d in PLANE:
            remote(ref, ref, xd_s.at[n], xd_r.at[n], c_at(d)).start()
        sent.append((part_of(n, 16 * (Z - 1)), xd_s.at[n]))

    def direct_pass(n):
        take(part_of(n, 16 * (Z - 1)), xd_r.at[n])
        cross(n)

    def lanes(h):
        return pl.ds(pl.multiple_of(LANE * h, LANE), LANE)

    def times(h, k, rows, r):
        total = jnp.dot(xg[0, r, rows], w_ref[k, 0:256, lanes(h)], preferred_element_type=jnp.float32)
        return total + jnp.dot(xg[1, r, rows], w_ref[k, 256:512, lanes(h)], preferred_element_type=jnp.float32)

    every, tail = slice(0, TOK), slice(TOK - 16, TOK)

    def chains(j, inner, body):
        last = j == HALF - 1

        @pl.loop(0, (2 if last else 4) * inner)
        def _(q):
            if last:
                h, i = q % 2, q // 2
                way = h
            else:
                way, h, i = q % 2, (q // 2) % 2, q // 4

            def pick(back):
                ups = (1 - h) * need_slot(HALF - j - back) + h * need_slot(HALF - 1 - j - back)
                downs = (1 - h) * need_slot(HALF + 1 + j - back) + h * need_slot(HALF + j - back)
                return (1 - way) * ups + way * downs

            body(way, h, i, pick)

    def a_hop(way, h, j, i):
        return remote(
            ring.at[h, way, j, i], ring.at[h, way, j + 1, i],
            a_s.at[h, way, i], a_r.at[h, way, j, i], z_at(1 - 2 * way),
        )

    def b_hop(way, h, j, p):
        rows = pl.ds(*QROWS[p])
        return remote(
            qring.at[h, way, j, rows], qring.at[h, way, j + 1, rows],
            b_s.at[h, way, p], b_r.at[h, way, j, p], z_at(1 - 2 * way),
        )

    def a_launch(starts, r):
        for way, h in starts:

            @pl.loop(0, 2)
            def _(i):
                ring[h, way, 0, i] = coded(times(h, i + 1, every, r))
                a_hop(way, h, 0, i).start()

    def a_compute(j):
        def body(way, h, i, pick):
            part[h, way, i] = times(h, i + 1, every, pick(0))

        chains(j, 2, body)

    def a_forward(j):
        def body(way, h, i, pick):
            a_hop(way, h, j - 1, i).wait()
            ring[h, way, j, i] = coded(plain(ring[h, way, j, i]) + part[h, way, i])
            a_hop(way, h, j, i).start()

        chains(j, 2, body)

    def b_compute(j):
        def body(way, h, i, pick):
            qpart[h, way, 0:16] = times(h, 0, tail, pick(1))
            qpart[h, way, 16:EXT] = times(h, 0, every, pick(0))

        chains(j, 1, body)

    def b_forward(j):
        def body(way, h, i, pick):
            for p in range(2):
                rows = slice(QROWS[p][0], sum(QROWS[p]))
                if j == 0:
                    qring[h, way, j, rows] = coded(qpart[h, way, rows])
                else:
                    b_hop(way, h, j - 1, p).wait()
                    qring[h, way, j, rows] = coded(plain(qring[h, way, j, rows]) + qpart[h, way, rows])
                b_hop(way, h, j, p).start()

        chains(j, 1, body)

    def a_own():
        @pl.loop(0, 4)
        def _(q):
            own[q // 2, q % 2] = times(q // 2, q % 2 + 1, every, Z - 1)

    def b_own():
        @pl.loop(0, 2)
        def _(h):
            qown[h, 0:16] = times(h, 0, tail, need_slot(-1))
            qown[h, 16:EXT] = times(h, 0, every, Z - 1)

    def halo_copy():
        return remote(pad.at[:, :, pl.ds(TOK, 8)], halo, h_s.at[0], h_r.at[0], z_at(1))

    def a_settle():
        @pl.loop(0, 4)
        def _(q):
            h, i = q // 2, q % 2
            stops = (HALF - h, HALF - 1 + h)
            for way in range(2):
                a_hop(way, h, stops[way] - 1, i).wait()
            total = own[h, i] + plain(ring[h, 0, stops[0], i]) + plain(ring[h, 1, stops[1], i])
            pad[h, i, 8:, :] = total * (1.0 / SCALE)

        halo_copy().start()

    first = (z > 0).astype(jnp.float32)

    def part2(h):
        mixed = []
        for i in range(2):
            pad[h, i, 0:8, :] = halo[h, i] * first
            total = jnp.zeros((TOK, LANE), jnp.float32)
            for j in range(TAPS):
                total += sf_ref[i + 1, pl.ds(j, 1), lanes(h)] * pad[h, i, 8 - j : 8 - j + TOK, :]
            mixed.append(total)
        drive[h] = mixed[0] * mixed[1]
        r = rates_ref[:, lanes(h)]
        f8 = jnp.exp(-8.0 * r)
        steps = [jnp.broadcast_to(f8[m : m + 1, :], (8, LANE)) for m in range(MODES)]

        def one(g, states):
            d = drive[h, pl.ds(pl.multiple_of(g * 8, 8), 8), :]
            return tuple(s * f + d for s, f in zip(states, steps))

        states = lax.fori_loop(0, TOK // 8, one, tuple(jnp.zeros((8, LANE), jnp.float32) for _ in range(MODES)))
        left = 7.0 - lax.broadcasted_iota(jnp.int32, (8, LANE), 0).astype(jnp.float32)
        for m in range(MODES):
            weight = jnp.exp(-r[m : m + 1, :] * left)
            ends[pl.ds(m, 1), :] = jnp.sum(states[m] * weight, axis=0, keepdims=True)
        end = ends[...]
        est[z, h] = (end * jnp.abs(end)).astype(jnp.bfloat16)

    def states_out():
        for d in RING:
            remote(est.at[z], est.at[z], e_s.at[0], e_r.at[0], z_at(d)).start()
        sent.append((est.at[pl.ds(0, Z - 1)], e_s.at[0]))

    def part3():
        starts, gains = [], []
        for h in range(2):
            r = rates_ref[:, lanes(h)]
            block = jnp.exp(-float(TOK) * r)
            entering = jnp.zeros((MODES, LANE), jnp.float32)
            for s in range(Z - 1):
                square = est[s, h].astype(jnp.float32)
                end = square * lax.rsqrt(jnp.maximum(jnp.abs(square), 1e-37))
                entering = jnp.where(s < z, entering * block + end, entering)
            factor = jnp.exp(-r)
            scaled = res_ref[:, lanes(h)] * jnp.sqrt(1.0 - jnp.exp(-2.0 * r))
            starts += [entering[:8], entering[8:]]
            gains.append((factor[:8], factor[8:], scaled[:8], scaled[8:]))

        def one(g, states):
            states = list(states)
            base = pl.multiple_of(g * 8, 8)
            for t in range(8):
                for h, (fa, fb, sa, sb) in enumerate(gains):
                    d = drive[h, pl.ds(base + t, 1), :]
                    a = states[2 * h] * fa + d
                    b = states[2 * h + 1] * fb + d
                    states[2 * h : 2 * h + 2] = a, b
                    ysum[h, pl.ds(pl.multiple_of((base + t) * 8, 8), 8), :] = a * sa + b * sb
            return tuple(states)

        lax.fori_loop(0, TOK // 8, one, tuple(starts))
        for h in range(2):
            total = ysum[h, pl.ds(0, TOK, stride=8), :]
            for i in range(1, 8):
                total += ysum[h, pl.ds(i, TOK, stride=8), :]
            conv[h] = total + skip_ref[:, lanes(h)] * drive[h]

    def finish(h):
        stops = (HALF - h, HALF - 1 + h)
        for p in range(2):
            for way in range(2):
                b_hop(way, h, stops[way] - 1, p).wait()
            rows = slice(QROWS[p][0], sum(QROWS[p]))
            total = qown[h, rows] + plain(qring[h, 0, stops[0], rows]) + plain(qring[h, 1, stops[1], rows])
            qpad[rows] = total * (1.0 / SCALE)
        qpad[0:16] = qpad[0:16] * first
        query = jnp.zeros((TOK, LANE), jnp.float32)
        for j in range(TAPS):
            query += sf_ref[0, pl.ds(j, 1), lanes(h)] * qpad[16 - j : 16 - j + TOK, :]
        out_ref[:, LANE * h : LANE * (h + 1)] = (query * conv[h]).astype(jnp.bfloat16)

    along(0)
    along(1)
    along(2)
    direct(0)
    direct(1)
    along(3)
    along(4)
    along(5)
    along(6)
    xg[core, Z - 1, mine] = xp[z]
    for load in loads[1:]:
        load.wait()
    direct(2)
    direct_pass(0)
    direct_pass(1)
    crossed(0)
    a_launch(((0, 0), (1, 1)), need_slot(HALF))
    direct(3)
    crossed(1)
    a_launch(((1, 0),), need_slot(HALF + 1))
    a_launch(((0, 1),), need_slot(HALF - 1))
    direct(4)
    direct_pass(2)
    direct(5)
    direct(6)
    ready = {1: 2, 2: 3, 3: 4, 4: 5, 6: 6}
    for step in range(1, HALF + LAG + 1):
        if step in ready:
            crossed(ready[step])
        if step < HALF:
            a_compute(step)
            a_forward(step)
        if step + 1 in ready:
            direct_pass(ready[step + 1])
        if step == HALF:
            a_settle()
        if LAG <= step < HALF + LAG:
            b_compute(step - LAG)
            b_forward(step - LAG)
        if step == HALF - 1:
            a_own()
        if step == HALF:
            halo_copy().wait()
            part2(0)
            part2(1)
            states_out()
        if step == HALF + 1:
            b_own()
        if step == HALF + 2:
            take(est.at[pl.ds(0, Z - 1)], e_r.at[0])
            part3()
    finish(0)
    finish(1)
    for ref, sem in sent:
        take(ref, sem)


def per_device(inputs, w_in, short_filter, rates, residues, skip):
    dma = pltpu.SemaphoreType.DMA
    f32, bf16 = jnp.float32, jnp.bfloat16
    n = len(CHUNKS)
    args = (inputs, w_in, short_filter, rates, residues, skip.reshape(1, -1))
    return pl.pallas_call(
        kernel,
        out_shape=jax.ShapeDtypeStruct(inputs.shape, jnp.bfloat16),
        in_specs=[pl.BlockSpec(memory_space=pl.ANY)] * 6,
        out_specs=pl.BlockSpec(memory_space=pltpu.VMEM),
        scratch_shapes=[pltpu.VMEM(a.shape, a.dtype) for a in args]
        + [
            pltpu.VMEM((TOK, 256), bf16),
            pltpu.VMEM((Z, 16, 256), bf16),
            pltpu.VMEM((2, Z, TOK, 256), bf16),
            pltpu.VMEM((2, 2, HALF + 1, 2, TOK, LANE), bf16),
            pltpu.VMEM((2, 2, HALF + 1, EXT, LANE), bf16),
            pltpu.VMEM((2, 2, 2, TOK, LANE), f32),
            pltpu.VMEM((2, 2, EXT, LANE), f32),
            pltpu.VMEM((2, 2, TOK, LANE), f32),
            pltpu.VMEM((2, EXT, LANE), f32),
            pltpu.VMEM((2, 2, TOK + 8, LANE), f32),
            pltpu.VMEM((EXT, LANE), f32),
            pltpu.VMEM((2, 2, 8, LANE), f32),
            pltpu.VMEM((2, TOK, LANE), f32),
            pltpu.VMEM((2, TOK, LANE), f32),
            pltpu.VMEM((Z, 2, MODES, LANE), bf16),
            pltpu.VMEM((MODES, LANE), f32),
            pltpu.VMEM((2, TOK * 8, LANE), f32),
            dma((6,)), dma((1,)), dma((1,)), dma((n,)), dma((n,)), dma((n,)), dma((n,)),
            dma((n,)), dma((n,)),
            dma((2, 2, 2)), dma((2, 2, HALF, 2)), dma((2, 2, 2)), dma((2, 2, HALF, 2)),
            dma((1,)), dma((1,)), dma((1,)), dma((1,)),
        ],
        compiler_params=pltpu.CompilerParams(
            collective_id=0, has_side_effects=True, vmem_limit_bytes=60 * 2**20
        ),
    )(*args)


def solution(mesh):
    in_specs = (
        P("seq", "ch"),
        P(None, "seq", "ch"),
        P(None, None, "ch"),
        P(None, "ch"),
        P(None, "ch"),
        P("ch"),
    )
    return jax.shard_map(
        per_device, mesh=mesh, in_specs=in_specs, out_specs=P("seq", "ch"), check_vma=False
    )
```
